128 devices in a mesh: row: 16 (over y, x_lo, core), col: 8 (over x_hi, z).
Axes of the slice: x: 4 (x_hi: 2, x_lo: 2; x = x_hi * 2 + x_lo), y: 4, z: 4, core: 2. Of those that a mesh axis runs over, the one named last changes fastest.
Arguments:
- spectra: bfloat16 [2, 16, 16, 512, 1024], P(None, 'row', None, 'col'), may hold values from -200 to 200
- block_pairs: int32 [16, 2], replicated, may hold values from 0 to 15
- band_bins: int32 [1024], P('col'), may hold values from 0 to 4095
Outputs:
- correlations: float32 [16, 512, 12, 512], P('row', 'col')
The draws below stay inside these ranges and needn't reach their ends.
Inputs may be any that keep to these rules, and one draw needn't show every extreme that they name: `block_pairs`: each row names the row block and the column block of one pair; the two may be equal and blocks may repeat across pairs. `band_bins`: bins of a transform of 8192 samples; entries may repeat.
All inputs are finite; a program needn't handle non-finite values.
Results may differ from the reference program's by a relative error of at most 0.014.
Values may be sent and summed in bfloat16 or wider, within the bound.
No kernel may reach another device: no remote copies, remote signals or barrier semaphores. Data moves between devices by JAX's collectives and lax.ppermute only.
A program may use at most 128 MiB of HBM per device.

```python
import math
import jax
import jax.numpy as jnp
from jax import lax

BLK = 512
F = 1024
L = 8192
LAGS = 12
NBLK = 16
NPAIR = 16
SEG = 16
BANDS = 8
FB = 128


def draw_spectra(key, part):
    key = jax.random.fold_in(key, 11)
    subkeys = jax.random.split(key, 3)
    full_shape = (2, SEG, NBLK, BLK, F)
    channel_scale = jnp.exp(jax.random.uniform(subkeys[1], (1, SEG, NBLK, BLK, 1), jnp.float32, 0.0, math.log(10.0)))
    base_field = jax.random.truncated_normal(subkeys[0], -4.0, 4.0, full_shape, jnp.float32)
    bin_scale = jnp.exp(jax.random.uniform(subkeys[2], (1, SEG, 1, 1, F), jnp.float32, math.log(0.5), math.log(5.0)))
    return (base_field * channel_scale * bin_scale).astype(jnp.bfloat16)


def plant(entries, own_key, smallest, high):
    longest = entries.shape.index(max(entries.shape))
    spots = []
    for shift in (0, 1):
        where = [jax.random.randint(jax.random.fold_in(own_key, axis), (), 0, length) for axis, length in enumerate(entries.shape)]
        where[longest] = (where[longest] + shift) % entries.shape[longest]
        spots.append(tuple(where))
    return entries.at[spots[0]].set(smallest).at[spots[1]].set(high)


def setup_inputs(seed: int = 0) -> dict:
    seeds = jax.random.split(jax.random.key(seed), 4)
    return {
        "spectra": draw_spectra(jax.random.fold_in(seeds[3], 71), 0),
        "block_pairs": plant(jax.random.randint(seeds[1], (NPAIR, 2), 0, NBLK), jax.random.fold_in(seeds[1], 1), 0, NBLK - 1).astype(jnp.int32),
        "band_bins": plant(jax.random.randint(seeds[2], (F,), 0, L // 2), jax.random.fold_in(seeds[2], 1), 0, (L // 2) - 1).astype(jnp.int32),
    }


epsilon = 1e-06

def whiten(values_in):
    values = values_in.astype(jnp.float32)
    energy = lax.optimization_barrier(jnp.mean(lax.optimization_barrier(jnp.sum(values * values, axis=-4, keepdims=True)), axis=-1, keepdims=True))
    return (values * lax.rsqrt(energy + epsilon)).astype(jnp.bfloat16)

def phase_tables(band_bins, lag_offsets):
    steps_mod = jnp.mod(band_bins[None, :] * lag_offsets[:, None], L).astype(jnp.int32)
    angle = steps_mod.astype(jnp.float32) * (2.0 * math.pi / L)
    return (jnp.cos(angle), jnp.sin(angle))

def reference(spectra, block_pairs, band_bins):
    whitened = lax.map(whiten, jnp.moveaxis(spectra, 2, 0))
    lag_offsets = jnp.arange(LAGS, dtype=jnp.int32) - LAGS // 2
    cosine, sine_table = phase_tables(band_bins, lag_offsets)
    scaling = 1.0 / math.sqrt(SEG * F)

    def pair_corr(pair_row):
        left_block = whitened[pair_row[0]].astype(jnp.float32)
        right_block = whitened[pair_row[1]].astype(jnp.float32).reshape(2, SEG, BLK, BANDS, FB)

        def one_lag(tables):
            cos_row, sin_row = tables
            turned = jnp.stack([left_block[0] * cos_row - left_block[1] * sin_row, left_block[0] * sin_row + left_block[1] * cos_row]).astype(jnp.bfloat16)
            turned = turned.astype(jnp.float32).reshape(2, SEG, BLK, BANDS, FB)
            partial_value = (jnp.einsum('csabf,csdbf->bad', turned, right_block) * scaling).astype(jnp.bfloat16)
            partial_value = lax.optimization_barrier(partial_value)
            return lax.optimization_barrier(jnp.sum(partial_value.astype(jnp.float32), axis=0))
        per_lag = lax.map(one_lag, (cosine, sine_table))
        return jnp.moveaxis(per_lag, 0, 1)
    return lax.map(pair_corr, block_pairs)
```

```python
import math

import jax
import jax.numpy as jnp
from jax import lax
from jax.experimental import pallas as pl
from jax.experimental.pallas import tpu as pltpu
from jax.sharding import PartitionSpec as P

L = 8192
LAGS = 12
HALF = LAGS // 2
EPS = 1e-06

NZ = 4
CH = 64
FQ = 256
GROUP = 2
BF = jnp.bfloat16
F32 = jnp.float32


def pack_kernel(sel, first, second, out):
    for core, ref in enumerate((first, second)):
        re = ref[0, 0, 0].astype(F32)
        im = ref[1, 0, 0].astype(F32)
        energy = jnp.mean(re * re + im * im, axis=-1, keepdims=True)
        gain = lax.rsqrt(energy + EPS)
        for comp, val in enumerate((re, im)):
            white = (val * gain).astype(BF)
            for z in range(NZ):
                out[0, core, 0, z, comp, :, 0:128] = white[:, z * 128 : z * 128 + 128]
                out[0, core, 0, z, comp, :, 128:256] = white[:, (z + 4) * 128 : (z + 4) * 128 + 128]


def pack(spectra, sel):
    pairs = sel.shape[0]
    block = (2, 1, 1, CH, 1024)
    return pl.pallas_call(
        pack_kernel,
        grid_spec=pltpu.PrefetchScalarGridSpec(
            num_scalar_prefetch=1,
            grid=(pairs,),
            in_specs=[
                pl.BlockSpec(block, lambda p, sel: (0, 0, sel[p, 0], 0, 0)),
                pl.BlockSpec(block, lambda p, sel: (0, 0, sel[p, 1], 0, 0)),
            ],
            out_specs=pl.BlockSpec(
                (1, 2, 1, NZ, 2, CH, FQ), lambda p, sel: (p // 2, 0, p % 2, 0, 0, 0, 0)
            ),
        ),
        out_shape=jax.ShapeDtypeStruct((8, 2, 2, NZ, 2, CH, FQ), BF),
        compiler_params=pltpu.CompilerParams(vmem_limit_bytes=32 * 2**20),
        cost_estimate=pl.CostEstimate(flops=32 * 2**20, bytes_accessed=16 * 2**20, transcendentals=0),
        name="pack",
    )(sel, spectra, spectra)


def corr_kernel(where, left, right, cos_ref, sin_ref, o0, o1, o2, o3, acc, turned, flipped):
    step = pl.program_id(0)
    width = 2 * GROUP * FQ

    @pl.when(step == 0)
    def _():
        acc[...] = jnp.zeros_like(acc)

    for g in range(GROUP):
        for comp in range(2):
            col = (2 * g + comp) * FQ
            flipped[col : col + FQ, :] = right[g, 0, :, comp].reshape(NZ * CH, FQ).T

    def put(slot, g, dz, re, im):
        rows = slice(dz * CH, dz * CH + CH)
        turned[slot, rows, 2 * g * FQ : (2 * g + 1) * FQ] = re.astype(BF)
        turned[slot, rows, (2 * g + 1) * FQ : (2 * g + 2) * FQ] = im.astype(BF)

    def multiply(slot, lag):
        acc[lag] += jnp.dot(turned[slot], flipped[...], preferred_element_type=F32)

    for m in range(HALF + 1):
        plus = 2 * (m % 2)
        minus = plus + 1
        for g in range(GROUP):
            for dz in range(NZ):
                z = where[2 + dz]
                re = left[g, 0, z, 0]
                im = left[g, 0, z, 1]
                if m == 0:
                    put(plus, g, dz, re, im)
                    continue
                re = re.astype(F32)
                im = im.astype(F32)
                cos = cos_ref[m : m + 1, :]
                sin = sin_ref[m : m + 1, :]
                rc, rs, ic, isn = re * cos, re * sin, im * cos, im * sin
                put(minus, g, dz, rc + isn, ic - rs)
                if m < HALF:
                    put(plus, g, dz, rc - isn, rs + ic)
        if m == 0:
            multiply(plus, HALF)
            continue
        multiply(minus, HALF - m)
        if m < HALF:
            multiply(plus, HALF + m)

    @pl.when(step == pl.num_programs(0) - 1)
    def _():
        for dz, out in enumerate((o0, o1, o2, o3)):
            out[...] = (acc[:, dz * CH : dz * CH + CH, :] * (1.0 / 128.0)).astype(BF)


def corr(where, left, right, right_index, cosine, sine):
    segs = left.shape[0]
    block = (GROUP, 1, NZ, 2, CH, FQ)
    full = lambda s, where: (0, 0)
    piece = jax.ShapeDtypeStruct((LAGS, CH, NZ * CH), BF)
    return pl.pallas_call(
        corr_kernel,
        grid_spec=pltpu.PrefetchScalarGridSpec(
            num_scalar_prefetch=1,
            grid=(segs // GROUP,),
            in_specs=[
                pl.BlockSpec(block, lambda s, where: (s, where[0], 0, 0, 0, 0)),
                pl.BlockSpec(block, right_index),
                pl.BlockSpec(cosine.shape, full),
                pl.BlockSpec(sine.shape, full),
            ],
            out_specs=[pl.BlockSpec(piece.shape, lambda s, where: (0, 0, 0))] * NZ,
            scratch_shapes=[
                pltpu.VMEM((LAGS, NZ * CH, NZ * CH), F32),
                pltpu.VMEM((4, NZ * CH, 2 * GROUP * FQ), BF),
                pltpu.VMEM((2 * GROUP * FQ, NZ * CH), BF),
            ],
        ),
        out_shape=[piece] * NZ,
        compiler_params=pltpu.CompilerParams(vmem_limit_bytes=40 * 2**20),
        cost_estimate=pl.CostEstimate(flops=13 * 10**9, bytes_accessed=12 * 2**20, transcendentals=0),
        name="corr",
    )(where, left, right, cosine, sine)


def total_kernel(where, *refs):
    out = refs[-1]
    own, other = refs[:NZ], refs[NZ : 2 * NZ]
    width = NZ * CH
    for k, group in enumerate((own, other)):
        at = pl.multiple_of(where[k] * width, width)
        for t in range(LAGS):
            val = group[0][t].astype(F32)
            for ref in group[1:]:
                val = val + ref[t].astype(F32)
            out[0, :, t, pl.ds(at, width)] = val


def total(where, parts):
    shape = (1, CH, LAGS, 2 * NZ * CH)
    return pl.pallas_call(
        total_kernel,
        grid_spec=pltpu.PrefetchScalarGridSpec(
            num_scalar_prefetch=1,
            grid=(1,),
            in_specs=[pl.BlockSpec((LAGS, CH, NZ * CH), lambda i, where: (0, 0, 0))] * len(parts),
            out_specs=pl.BlockSpec(shape, lambda i, where: (0, 0, 0, 0)),
        ),
        out_shape=jax.ShapeDtypeStruct(shape, F32),
        compiler_params=pltpu.CompilerParams(vmem_limit_bytes=32 * 2**20),
        name="total",
    )(where, *parts)


def places():
    return [
        (y, xl, c, xh, z)
        for y in range(4)
        for xl in range(2)
        for c in range(2)
        for xh in range(2)
        for z in range(NZ)
    ]


def index(y, xl, c, xh, z):
    return ((y * 2 + xl) * 2 + c) * 8 + xh * 4 + z


def body(spectra, block_pairs, band_bins):
    both = ("row", "col")
    row = lax.axis_index("row")
    col = lax.axis_index("col")
    core = row % 2
    xh = col // 4
    z = col % 4

    sel = jnp.where(xh == 0, block_pairs[:, ::-1], block_pairs)
    packed = pack(spectra, sel).reshape(128, 2, CH, FQ)
    landed = lax.all_to_all(packed, both, split_axis=0, concat_axis=0, tiled=True)
    landed = landed.reshape(16, 2, NZ, 2, CH, FQ)

    bins_there = lax.ppermute(
        band_bins, both, [(index(*p), index(p[0], p[1], p[2], 1 - p[3], p[4])) for p in places()]
    )
    bins = jnp.where(
        xh == 0,
        jnp.concatenate([band_bins, bins_there]),
        jnp.concatenate([bins_there, band_bins]),
    )
    steps = jnp.arange(8, dtype=jnp.int32)
    angle = jnp.mod(bins[None, :] * steps[:, None], L).astype(F32) * (2.0 * math.pi / L)
    cosine, sine = jnp.cos(angle), jnp.sin(angle)

    where = jnp.stack([1 - core, core] + [(z + dz) % NZ for dz in range(NZ)]).astype(jnp.int32)
    mine = lax.dynamic_slice_in_dim(landed, core, 1, axis=1)
    theirs = lax.ppermute(
        mine, both, [(index(*p), index(p[0], p[1], 1 - p[2], p[3], p[4])) for p in places()]
    )

    def send(parts):
        return [
            lax.ppermute(
                part,
                both,
                [(index(*p), index(p[0], p[1], p[3], 1 - p[2], (p[4] + dz) % NZ)) for p in places()],
            )
            for dz, part in enumerate(parts)
        ]

    first = corr(where, landed, landed, lambda s, where: (s, where[1], 0, 0, 0, 0), cosine, sine)
    sent_first = send(first)
    second = corr(where, landed, theirs, lambda s, where: (s, 0, 0, 0, 0, 0), cosine, sine)
    sent_second = send(second)
    halves = jnp.stack([1 - xh, xh]).astype(jnp.int32)
    return total(halves, sent_first + sent_second)


def solution(mesh):
    in_specs = (P(None, "row", None, "col", None), P(), P("col"))
    out_specs = P("row", "col", None, None)
    return jax.shard_map(body, mesh=mesh, in_specs=in_specs, out_specs=out_specs, check_vma=False)
```

```python
import functools
import math

import jax
import jax.numpy as jnp
from jax import lax
from jax.experimental import pallas as pl
from jax.experimental.pallas import tpu as pltpu
from jax.sharding import PartitionSpec as P

L = 8192
LAGS = 12
HALF = LAGS // 2
EPS = 1e-06

NZ = 4
CH = 64
FB = 128
NB = 1024 // FB
BF = jnp.bfloat16
F32 = jnp.float32


def pack_kernel(group, sel, block, low, high, white, sems):
    step = pl.program_id(0)
    for g in range(group):
        re = block[0, 0, g].astype(F32)
        im = block[1, 0, g].astype(F32)
        energy = jnp.mean(re * re + im * im, axis=-1, keepdims=True)
        gain = lax.rsqrt(energy + EPS)
        for comp, val in enumerate((re, im)):
            scaled = (val * gain).astype(BF)
            for k in range(NB):
                white[step * group + g, k, comp] = scaled[:, k * FB : (k + 1) * FB]

    def copies(pair, core):
        return [
            pltpu.make_async_copy(
                white.at[sel[pair, core], pl.ds(part * NZ, NZ)],
                out.at[pair // 2, core, pair % 2],
                sems.at[part, pair, core],
            )
            for part, out in enumerate((low, high))
        ]

    for pair in range(16):
        for core in range(2):

            @pl.when(sel[pair, core] // group == step)
            def _(pair=pair, core=core):
                for copy in copies(pair, core):
                    copy.start()

    @pl.when(step == pl.num_programs(0) - 1)
    def _():
        for pair in range(16):
            for core in range(2):
                for copy in copies(pair, core):
                    copy.wait()


def pack(spectra, sel):
    blocks = spectra.shape[2]
    group = 4
    out = jax.ShapeDtypeStruct((8, 2, 2, NZ, 2, CH, FB), BF)
    return pl.pallas_call(
        functools.partial(pack_kernel, group),
        grid_spec=pltpu.PrefetchScalarGridSpec(
            num_scalar_prefetch=1,
            grid=(blocks // group,),
            in_specs=[pl.BlockSpec((2, 1, group, CH, 1024), lambda p, sel: (0, 0, p, 0, 0))],
            out_specs=[pl.BlockSpec(memory_space=pl.ANY)] * 2,
            scratch_shapes=[
                pltpu.VMEM((blocks, NB, 2, CH, FB), BF),
                pltpu.SemaphoreType.DMA((2, 16, 2)),
            ],
        ),
        out_shape=[out] * 2,
        compiler_params=pltpu.CompilerParams(vmem_limit_bytes=60 * 2**20),
        cost_estimate=pl.CostEstimate(flops=16 * 2**20, bytes_accessed=12 * 2**20, transcendentals=0),
        name="pack",
    )(sel, spectra)


def turn_and_multiply(group, where, left, rights, cos_ref, sin_ref, even, odd, flipped, add):
    rows_all = NZ * CH

    def col(g, comp):
        return slice((2 * g + comp) * FB, (2 * g + comp + 1) * FB)

    for g in range(group):
        for comp in range(2):
            for h, right in enumerate(rights):
                block = right[g, 0, :, comp].reshape(rows_all, FB)
                flipped[col(g, comp), h * rows_all : (h + 1) * rows_all] = block.T

    def turn(m, turned, both):
        cos = jnp.broadcast_to(cos_ref[pl.ds(m, 1), :], (CH, FB)).astype(BF)
        sin = jnp.broadcast_to(sin_ref[pl.ds(m, 1), :], (CH, FB)).astype(BF)
        for g in range(group):
            for dz in range(NZ):
                z = where[2 + dz]
                re = left[g, 0, z, 0]
                im = left[g, 0, z, 1]
                rc, rs, ic, isn = re * cos, re * sin, im * cos, im * sin
                rows = slice(dz * CH, dz * CH + CH)
                more = slice(rows_all + dz * CH, rows_all + dz * CH + CH)
                turned[rows, col(g, 0)] = rc + isn
                turned[rows, col(g, 1)] = ic - rs
                turned[more, col(g, 0)] = rc - isn if both else re
                turned[more, col(g, 1)] = rs + ic if both else im

    def multiply(m, turned):
        product = jnp.dot(turned[...], flipped[...], preferred_element_type=F32)
        add(HALF - m if isinstance(m, int) else jnp.where(m == 0, 0, HALF - m), product[:rows_all])
        add(HALF + m, product[rows_all:])

    turn(HALF, even, False)

    def step(i, carry):
        m = 2 * i + 1
        turn(m, odd, True)
        multiply(m - 1, even)
        turn(m + 1, even, True)
        multiply(m, odd)
        return carry

    lax.fori_loop(0, 2, step, 0)
    turn(HALF - 1, odd, True)
    multiply(HALF - 2, even)
    multiply(HALF - 1, odd)


def first_kernel(group, where, left, own, other, cos_ref, sin_ref, own_sum, other_sum, even, odd, flipped):
    @pl.when(pl.program_id(0) == 0)
    def _():
        own_sum[...] = jnp.zeros_like(own_sum)
        other_sum[...] = jnp.zeros_like(other_sum)

    def add(lag, product):
        own_sum[lag] += product[:, : NZ * CH]
        other_sum[lag] += product[:, NZ * CH :]

    turn_and_multiply(group, where, left, (own, other), cos_ref, sin_ref, even, odd, flipped, add)


def second_kernel(group, where, left, right, cos_ref, sin_ref, before, o0, o1, o2, o3, even, odd, flipped):
    def add(lag, product):
        for dz, out in enumerate((o0, o1, o2, o3)):
            rows = slice(dz * CH, dz * CH + CH)
            out[lag] = ((before[lag, rows] + product[rows]) * (1.0 / 128.0)).astype(BF)

    turn_and_multiply(group, where, left, (right,), cos_ref, sin_ref, even, odd, flipped, add)


SUMS = (LAGS, NZ * CH, NZ * CH)


def spec(group, at=None):
    index_map = (lambda s, where: (s, 0, 0, 0, 0, 0)) if at is None else (lambda s, where: (s, where[at], 0, 0, 0, 0))
    return pl.BlockSpec((group, 1, NZ, 2, CH, FB), index_map)


def table_spec():
    return pl.BlockSpec((8, FB), lambda s, where: (0, 0))


def whole(shape):
    return pl.BlockSpec(shape, lambda s, where: (0, 0, 0))


def first_half(where, landed, theirs, cosine, sine):
    group = 8
    return pl.pallas_call(
        functools.partial(first_kernel, group),
        grid_spec=pltpu.PrefetchScalarGridSpec(
            num_scalar_prefetch=1,
            grid=(landed.shape[0] // group,),
            in_specs=[spec(group, 0), spec(group, 1), spec(group), table_spec(), table_spec()],
            out_specs=[whole(SUMS)] * 2,
            scratch_shapes=[
                pltpu.VMEM((2 * NZ * CH, 2 * group * FB), BF),
                pltpu.VMEM((2 * NZ * CH, 2 * group * FB), BF),
                pltpu.VMEM((2 * group * FB, 2 * NZ * CH), BF),
            ],
        ),
        out_shape=[jax.ShapeDtypeStruct(SUMS, F32)] * 2,
        compiler_params=pltpu.CompilerParams(vmem_limit_bytes=40 * 2**20),
        cost_estimate=pl.CostEstimate(flops=13 * 10**9, bytes_accessed=12 * 2**20, transcendentals=0),
        name="first_half",
    )(where, landed, landed, theirs, cosine, sine)


def second_half(where, landed, right, at, cosine, sine, before):
    group = landed.shape[0]
    piece = jax.ShapeDtypeStruct((LAGS, CH, NZ * CH), BF)
    return pl.pallas_call(
        functools.partial(second_kernel, group),
        grid_spec=pltpu.PrefetchScalarGridSpec(
            num_scalar_prefetch=1,
            grid=(1,),
            in_specs=[spec(group, 0), spec(group, at), table_spec(), table_spec(), whole(SUMS)],
            out_specs=[whole(piece.shape)] * NZ,
            scratch_shapes=[
                pltpu.VMEM((2 * NZ * CH, 2 * group * FB), BF),
                pltpu.VMEM((2 * NZ * CH, 2 * group * FB), BF),
                pltpu.VMEM((2 * group * FB, NZ * CH), BF),
            ],
        ),
        out_shape=[piece] * NZ,
        compiler_params=pltpu.CompilerParams(vmem_limit_bytes=40 * 2**20),
        cost_estimate=pl.CostEstimate(flops=65 * 10**8, bytes_accessed=8 * 2**20, transcendentals=0),
        name="second_half",
    )(where, landed, right, cosine, sine, before)


def total_kernel(where, *refs):
    out = refs[-1]
    own, other = refs[:NZ], refs[NZ : 2 * NZ]
    width = NZ * CH
    for k, group in enumerate((own, other)):
        at = pl.multiple_of(where[k] * width, width)
        for t in range(LAGS):
            val = group[0][t].astype(F32)
            for ref in group[1:]:
                val = val + ref[t].astype(F32)
            out[0, t, :, pl.ds(at, width)] = val


def total(where, parts):
    shape = (1, LAGS, CH, 2 * NZ * CH)
    return pl.pallas_call(
        total_kernel,
        grid_spec=pltpu.PrefetchScalarGridSpec(
            num_scalar_prefetch=1,
            grid=(1,),
            in_specs=[pl.BlockSpec((LAGS, CH, NZ * CH), lambda i, where: (0, 0, 0))] * len(parts),
            out_specs=pl.BlockSpec(shape, lambda i, where: (0, 0, 0, 0)),
        ),
        out_shape=jax.ShapeDtypeStruct(shape, F32),
        compiler_params=pltpu.CompilerParams(vmem_limit_bytes=32 * 2**20),
        name="total",
    )(where, *parts)


def places():
    return [
        (y, xl, c, xh, z)
        for y in range(4)
        for xl in range(2)
        for c in range(2)
        for xh in range(2)
        for z in range(NZ)
    ]


def index(y, xl, c, xh, z):
    return ((y * 2 + xl) * 2 + c) * 8 + xh * 4 + z


def body(spectra, block_pairs, band_bins):
    both = ("row", "col")
    row = lax.axis_index("row")
    col = lax.axis_index("col")
    core = row % 2
    xh = col // 4
    z = col % 4

    bins_there = lax.ppermute(
        band_bins, both, [(index(*p), index(p[0], p[1], p[2], 1 - p[3], p[4])) for p in places()]
    )
    low = jnp.where(xh == 0, band_bins, bins_there)
    high = jnp.where(xh == 0, bins_there, band_bins)
    steps = jnp.arange(8, dtype=jnp.int32)
    angle = jnp.mod(jnp.stack([low, high])[:, None, :] * steps[:, None], L).astype(F32) * (2.0 * math.pi / L)
    cosine, sine = jnp.cos(angle), jnp.sin(angle)

    sel = jnp.where(xh == 0, block_pairs[:, ::-1], block_pairs)
    where = jnp.stack([1 - core, core] + [(z + dz) % NZ for dz in range(NZ)]).astype(jnp.int32)
    halves = jnp.stack([1 - xh, xh]).astype(jnp.int32)

    def swap(mine):
        return lax.ppermute(
            mine, both, [(index(*p), index(p[0], p[1], 1 - p[2], p[3], p[4])) for p in places()]
        )

    def exchange(packed):
        landed = lax.all_to_all(packed.reshape(128, 2, CH, FB), both, split_axis=0, concat_axis=0, tiled=True)
        landed = landed.reshape(16, 2, NZ, 2, CH, FB)
        return landed, swap(lax.dynamic_slice_in_dim(landed, core, 1, axis=1))

    def send(parts):
        return [
            lax.ppermute(
                part,
                both,
                [(index(*p), index(p[0], p[1], p[3], 1 - p[2], (p[4] + dz) % NZ)) for p in places()],
            )
            for dz, part in enumerate(parts)
        ]

    packed0, packed1 = pack(spectra, sel)
    packed1, cosine, sine, where, halves = lax.optimization_barrier((packed1, cosine, sine, where, halves))
    landed0, theirs0 = exchange(packed0)
    own, other = first_half(where, landed0, theirs0, cosine[0], sine[0])
    landed1 = lax.all_to_all(packed1.reshape(128, 2, CH, FB), both, split_axis=0, concat_axis=0, tiled=True)
    landed1, own, other = lax.optimization_barrier((landed1, own, other))
    landed1 = landed1.reshape(16, 2, NZ, 2, CH, FB)
    theirs1 = swap(lax.dynamic_slice_in_dim(landed1, core, 1, axis=1))
    first = send(second_half(where, landed1, landed1, 1, cosine[1], sine[1], own))
    second = send(second_half(where, landed1, theirs1, None, cosine[1], sine[1], other))
    return jnp.transpose(total(halves, first + second), (0, 2, 1, 3))


def solution(mesh):
    in_specs = (P(None, "row", None, "col", None), P(), P("col"))
    out_specs = P("row", "col", None, None)
    return jax.shard_map(body, mesh=mesh, in_specs=in_specs, out_specs=out_specs, check_vma=False)
```

```python
import functools
import math

import jax
import jax.numpy as jnp
from jax import lax
from jax.experimental import pallas as pl
from jax.experimental.pallas import tpu as pltpu
from jax.sharding import PartitionSpec as P

L = 8192
LAGS = 12
HALF = LAGS // 2
EPS = 1e-06

NZ = 4
CH = 64
FB = 128
CHUNKS = ((0, 0, 6), (1, 0, 6))
HOPS = (2, 1, 3, 0)
BF = jnp.bfloat16
F32 = jnp.float32


def pack_kernel(group, part, pairs, xh, block, out, white, sems):
    step = pl.program_id(0)
    for g in range(group):
        re = block[0, 0, g].astype(F32)
        im = block[1, 0, g].astype(F32)
        energy = jnp.mean(re * re + im * im, axis=-1, keepdims=True)
        gain = lax.rsqrt(energy + EPS)
        for comp, val in enumerate((re, im)):
            for z in range(NZ):
                at = (part * NZ + z) * FB
                white[step * group + g, z, comp] = (val[:, at : at + FB] * gain).astype(BF)

    def chosen(pair, core):
        return pairs[jnp.where(xh[0] == core, 1, 0), pair]

    def copy(pair, core):
        return pltpu.make_async_copy(
            white.at[chosen(pair, core)], out.at[pair // 2, core, pair % 2], sems.at[pair, core]
        )

    for pair in range(16):
        for core in range(2):

            @pl.when(chosen(pair, core) // group == step)
            def _(pair=pair, core=core):
                copy(pair, core).start()

    @pl.when(step == pl.num_programs(0) - 1)
    def _():
        for pair in range(16):
            for core in range(2):
                copy(pair, core).wait()


def pack(spectra, pairs, xh, part):
    blocks = spectra.shape[2]
    group = 4
    return pl.pallas_call(
        functools.partial(pack_kernel, group, part),
        grid_spec=pltpu.PrefetchScalarGridSpec(
            num_scalar_prefetch=2,
            grid=(blocks // group,),
            in_specs=[pl.BlockSpec((2, 1, group, CH, 1024), lambda p, pairs, xh: (0, 0, p, 0, 0))],
            out_specs=pl.BlockSpec(memory_space=pl.ANY),
            scratch_shapes=[
                pltpu.VMEM((blocks, NZ, 2, CH, FB), BF),
                pltpu.SemaphoreType.DMA((16, 2)),
            ],
        ),
        out_shape=jax.ShapeDtypeStruct((8, 2, 2, NZ, 2, CH, FB), BF),
        compiler_params=pltpu.CompilerParams(vmem_limit_bytes=60 * 2**20),
        cost_estimate=pl.CostEstimate(flops=16 * 2**20, bytes_accessed=8 * 2**20, transcendentals=0),
        name="pack",
    )(pairs, xh, spectra)


def turn_and_multiply(group, first, count, where, left, rights, cos_ref, sin_ref, even, odd, flat, add):
    rows_all = NZ * CH

    def col(g, comp):
        return slice((2 * g + comp) * FB, (2 * g + comp + 1) * FB)

    for h, right in enumerate(rights):
        for g in range(group):
            for comp in range(2):
                for z in range(NZ):
                    flat[h * rows_all + z * CH : h * rows_all + (z + 1) * CH, col(g, comp)] = right[g, 0, z, comp]

    def turn(m, turned):
        lag = HALF if isinstance(m, int) and m == 0 else m
        both = lag is m
        cos = jnp.broadcast_to(cos_ref[pl.ds(lag, 1), :], (CH, FB)).astype(BF)
        sin = jnp.broadcast_to(sin_ref[pl.ds(lag, 1), :], (CH, FB)).astype(BF)
        for g in range(group):
            for dz in range(NZ):
                z = where[2 + dz]
                re = left[g, 0, z, 0]
                im = left[g, 0, z, 1]
                rc, rs, ic, isn = re * cos, re * sin, im * cos, im * sin
                rows = slice(dz * CH, dz * CH + CH)
                more = slice(rows_all + dz * CH, rows_all + dz * CH + CH)
                turned[rows, col(g, 0)] = rc + isn
                turned[rows, col(g, 1)] = ic - rs
                turned[more, col(g, 0)] = rc - isn if both else re
                turned[more, col(g, 1)] = rs + ic if both else im

    def multiply(m, turned):
        product = lax.dot_general(
            turned[...], flat[...], (((1,), (1,)), ((), ())), preferred_element_type=F32
        )
        add(2 * (m - first), product[:rows_all])
        add(2 * (m - first) + 1, product[rows_all:])

    turn(first, even)
    loops = (count - 2) // 2 if count > 4 else 0

    def step(i, carry):
        m = first + 2 * i + 1
        turn(m, odd)
        multiply(m - 1, even)
        turn(m + 1, even)
        multiply(m, odd)
        return carry

    if loops:
        lax.fori_loop(0, loops, step, 0)
    now, later = even, odd
    for m in range(first + 2 * loops, first + count):
        if m + 1 < first + count:
            turn(m + 1, later)
        multiply(m, now)
        now, later = later, now


def first_kernel(group, where, left, own, other, cos_ref, sin_ref, own_sum, other_sum, even, odd, flat):
    @pl.when(pl.program_id(0) == 0)
    def _():
        own_sum[...] = jnp.zeros_like(own_sum)
        other_sum[...] = jnp.zeros_like(other_sum)

    def add(at, product):
        own_sum[at] += product[:, : NZ * CH]
        other_sum[at] += product[:, NZ * CH :]

    turn_and_multiply(group, 0, HALF, where, left, (own, other), cos_ref, sin_ref, even, odd, flat, add)


def second_kernel(group, first, count, where, left, right, cos_ref, sin_ref, before, o0, o1, o2, o3, even, odd, flat):
    def add(at, product):
        for dz, out in enumerate((o0, o1, o2, o3)):
            rows = slice(dz * CH, dz * CH + CH)
            out[at] = ((before[at, rows] + product[rows]) * (1.0 / 128.0)).astype(BF)

    turn_and_multiply(group, first, count, where, left, (right,), cos_ref, sin_ref, even, odd, flat, add)


SUMS = (LAGS, NZ * CH, NZ * CH)


def spec(group, at=None):
    index_map = (lambda s, where: (s, 0, 0, 0, 0, 0)) if at is None else (lambda s, where: (s, where[at], 0, 0, 0, 0))
    return pl.BlockSpec((group, 1, NZ, 2, CH, FB), index_map)


def table_spec():
    return pl.BlockSpec((8, FB), lambda s, where: (0, 0))


def whole(shape, at=0):
    return pl.BlockSpec(shape, lambda s, where: (at, 0, 0))


def first_half(where, landed, theirs, cosine, sine):
    group = 8
    return pl.pallas_call(
        functools.partial(first_kernel, group),
        grid_spec=pltpu.PrefetchScalarGridSpec(
            num_scalar_prefetch=1,
            grid=(landed.shape[0] // group,),
            in_specs=[spec(group, 0), spec(group, 1), spec(group), table_spec(), table_spec()],
            out_specs=[whole(SUMS)] * 2,
            scratch_shapes=[
                pltpu.VMEM((2 * NZ * CH, 2 * group * FB), BF),
                pltpu.VMEM((2 * NZ * CH, 2 * group * FB), BF),
                pltpu.VMEM((2 * NZ * CH, 2 * group * FB), BF),
            ],
        ),
        out_shape=[jax.ShapeDtypeStruct(SUMS, F32)] * 2,
        compiler_params=pltpu.CompilerParams(vmem_limit_bytes=40 * 2**20),
        cost_estimate=pl.CostEstimate(flops=13 * 10**9, bytes_accessed=12 * 2**20, transcendentals=0),
        name="first_half",
    )(where, landed, landed, theirs, cosine, sine)


def second_half(where, landed, right, at, cosine, sine, before, first=0, count=HALF):
    group = landed.shape[0]
    piece = jax.ShapeDtypeStruct((2 * count, CH, NZ * CH), BF)
    return pl.pallas_call(
        functools.partial(second_kernel, group, first, count),
        grid_spec=pltpu.PrefetchScalarGridSpec(
            num_scalar_prefetch=1,
            grid=(1,),
            in_specs=[spec(group, 0), spec(group, at), table_spec(), table_spec(), whole((2 * count, *SUMS[1:]), first // count)],
            out_specs=[whole(piece.shape)] * NZ,
            scratch_shapes=[
                pltpu.VMEM((2 * NZ * CH, 2 * group * FB), BF),
                pltpu.VMEM((2 * NZ * CH, 2 * group * FB), BF),
                pltpu.VMEM((NZ * CH, 2 * group * FB), BF),
            ],
        ),
        out_shape=[piece] * NZ,
        compiler_params=pltpu.CompilerParams(vmem_limit_bytes=40 * 2**20),
        cost_estimate=pl.CostEstimate(flops=count * 11 * 10**8, bytes_accessed=8 * 2**20, transcendentals=0),
        name="second_half",
    )(where, landed, right, cosine, sine, before)


def total_kernel(chunks, where, *refs):
    out = refs[-1]
    width = NZ * CH
    for k, (half, first, count) in enumerate(chunks):
        at = pl.multiple_of(where[half] * width, width)
        group = refs[k * NZ : (k + 1) * NZ]
        for m in range(first, first + count):
            for sign in range(2):
                i = 2 * (m - first) + sign
                val = group[0][i].astype(F32)
                for ref in group[1:]:
                    val = val + ref[i].astype(F32)
                lag = HALF + m if sign else (HALF - m if m else 0)
                out[0, lag, :, pl.ds(at, width)] = val


def total(where, chunks, parts):
    shape = (1, LAGS, CH, 2 * NZ * CH)
    return pl.pallas_call(
        functools.partial(total_kernel, chunks),
        grid_spec=pltpu.PrefetchScalarGridSpec(
            num_scalar_prefetch=1,
            grid=(1,),
            in_specs=[pl.BlockSpec(part.shape, lambda i, where: (0, 0, 0)) for part in parts],
            out_specs=pl.BlockSpec(shape, lambda i, where: (0, 0, 0, 0)),
        ),
        out_shape=jax.ShapeDtypeStruct(shape, F32),
        compiler_params=pltpu.CompilerParams(vmem_limit_bytes=32 * 2**20),
        name="total",
    )(where, *parts)


def places():
    return [
        (y, xl, c, xh, z)
        for y in range(4)
        for xl in range(2)
        for c in range(2)
        for xh in range(2)
        for z in range(NZ)
    ]


def index(y, xl, c, xh, z):
    return ((y * 2 + xl) * 2 + c) * 8 + xh * 4 + z


def body(spectra, block_pairs, band_bins):
    both = ("row", "col")
    row = lax.axis_index("row")
    col = lax.axis_index("col")
    core = row % 2
    xh = col // 4
    z = col % 4

    bins_there = lax.ppermute(
        band_bins, both, [(index(*p), index(p[0], p[1], p[2], 1 - p[3], p[4])) for p in places()]
    )
    low = jnp.where(xh == 0, band_bins, bins_there)
    high = jnp.where(xh == 0, bins_there, band_bins)
    steps = jnp.arange(8, dtype=jnp.int32)
    angle = jnp.mod(jnp.stack([low, high])[:, None, :] * steps[:, None], L).astype(F32) * (2.0 * math.pi / L)
    cosine, sine = jnp.cos(angle), jnp.sin(angle)

    where = jnp.stack([1 - core, core] + [(z + hop) % NZ for hop in HOPS]).astype(jnp.int32)
    halves = jnp.stack([1 - xh, xh]).astype(jnp.int32)

    def swap(mine):
        return lax.ppermute(
            mine, both, [(index(*p), index(p[0], p[1], 1 - p[2], p[3], p[4])) for p in places()]
        )

    def exchange(packed):
        landed = lax.all_to_all(packed.reshape(128, 2, CH, FB), both, split_axis=0, concat_axis=0, tiled=True)
        landed = landed.reshape(16, 2, NZ, 2, CH, FB)
        return landed, swap(lax.dynamic_slice_in_dim(landed, core, 1, axis=1))

    def send(parts):
        return [
            lax.ppermute(
                part,
                both,
                [(index(*p), index(p[0], p[1], p[3], 1 - p[2], (p[4] + hop) % NZ)) for p in places()],
            )
            for hop, part in zip(HOPS, parts)
        ]

    pairs, side = block_pairs.T, xh.reshape(1)
    packed0 = pack(spectra, pairs, side, 0)
    packed1 = pack(spectra, pairs, side, 1)
    packed1, cosine, sine, where, halves = lax.optimization_barrier((packed1, cosine, sine, where, halves))
    landed0, theirs0 = exchange(packed0)
    own, other = first_half(where, landed0, theirs0, cosine[0], sine[0])
    landed1 = lax.all_to_all(packed1.reshape(128, 2, CH, FB), both, split_axis=0, concat_axis=0, tiled=True)
    landed1, own, other = lax.optimization_barrier((landed1, own, other))
    landed1 = landed1.reshape(16, 2, NZ, 2, CH, FB)
    theirs1 = swap(lax.dynamic_slice_in_dim(landed1, core, 1, axis=1))
    chunks = CHUNKS
    parts = []
    for half, first, count in chunks:
        right, at, before = (landed1, 1, own) if half == 0 else (theirs1, None, other)
        parts += send(second_half(where, landed1, right, at, cosine[1], sine[1], before, first, count))
    return jnp.transpose(total(halves, chunks, parts), (0, 2, 1, 3))


def solution(mesh):
    in_specs = (P(None, "row", None, "col", None), P(), P("col"))
    out_specs = P("row", "col", None, None)
    return jax.shard_map(body, mesh=mesh, in_specs=in_specs, out_specs=out_specs, check_vma=False)
```

```python
import functools
import math

import jax
import jax.numpy as jnp
from jax import lax
from jax.experimental import pallas as pl
from jax.experimental.pallas import tpu as pltpu
from jax.sharding import PartitionSpec as P

L = 8192
LAGS = 12
HALF = LAGS // 2
EPS = 1e-06

NZ = 4
CH = 64
FB = 128
HOPS = (2, 1, 3, 0)
BF = jnp.bfloat16
F32 = jnp.float32


def pack_kernel(group, part, pairs, xh, block, out, white, sems):
    step = pl.program_id(0)
    for g in range(group):
        re = block[0, 0, g].astype(F32)
        im = block[1, 0, g].astype(F32)
        energy = jnp.mean(re * re + im * im, axis=-1, keepdims=True)
        gain = lax.rsqrt(energy + EPS)
        for comp, val in enumerate((re, im)):
            for z in range(NZ):
                at = (part * NZ + z) * FB
                white[step * group + g, z, comp] = (val[:, at : at + FB] * gain).astype(BF)

    def chosen(pair, core):
        return pairs[jnp.where(xh[0] == core, 1, 0), pair]

    def copy(pair, core):
        return pltpu.make_async_copy(
            white.at[chosen(pair, core)], out.at[pair // 2, core, pair % 2], sems.at[pair, core]
        )

    for pair in range(16):
        for core in range(2):

            @pl.when(chosen(pair, core) // group == step)
            def _(pair=pair, core=core):
                copy(pair, core).start()

    @pl.when(step == pl.num_programs(0) - 1)
    def _():
        for pair in range(16):
            for core in range(2):
                copy(pair, core).wait()


def pack(spectra, pairs, xh, part):
    blocks = spectra.shape[2]
    group = 4
    return pl.pallas_call(
        functools.partial(pack_kernel, group, part),
        grid_spec=pltpu.PrefetchScalarGridSpec(
            num_scalar_prefetch=2,
            grid=(blocks // group,),
            in_specs=[pl.BlockSpec((2, 1, group, CH, 1024), lambda p, pairs, xh: (0, 0, p, 0, 0))],
            out_specs=pl.BlockSpec(memory_space=pl.ANY),
            scratch_shapes=[
                pltpu.VMEM((blocks, NZ, 2, CH, FB), BF),
                pltpu.SemaphoreType.DMA((16, 2)),
            ],
        ),
        out_shape=jax.ShapeDtypeStruct((8, 2, 2, NZ, 2, CH, FB), BF),
        compiler_params=pltpu.CompilerParams(vmem_limit_bytes=60 * 2**20),
        cost_estimate=pl.CostEstimate(flops=16 * 2**20, bytes_accessed=8 * 2**20, transcendentals=0),
        name="pack",
    )(pairs, xh, spectra)


def col(g, comp):
    return slice((2 * g + comp) * FB, (2 * g + comp + 1) * FB)


def turn_and_multiply(group, where, left, cos_ref, sin_ref, even, odd, flat, add, arrive=None, ready=None):
    rows_all = NZ * CH

    def turn(m, turned, arrive=None):
        lag = HALF if isinstance(m, int) and m == 0 else m
        both = lag is m
        cos = jnp.broadcast_to(cos_ref[pl.ds(lag, 1), :], (CH, FB)).astype(BF)
        sin = jnp.broadcast_to(sin_ref[pl.ds(lag, 1), :], (CH, FB)).astype(BF)
        for g in range(group):
            if arrive is not None:
                arrive(g)
            for dz in range(NZ):
                z = where[2 + dz]
                re = left[g, 0, z, 0]
                im = left[g, 0, z, 1]
                rc, rs, ic, isn = re * cos, re * sin, im * cos, im * sin
                rows = slice(dz * CH, dz * CH + CH)
                more = slice(rows_all + dz * CH, rows_all + dz * CH + CH)
                turned[rows, col(g, 0)] = rc + isn
                turned[rows, col(g, 1)] = ic - rs
                turned[more, col(g, 0)] = rc - isn if both else re
                turned[more, col(g, 1)] = rs + ic if both else im

    def multiply(m, turned):
        product = lax.dot_general(
            turned[...], flat[...].reshape(-1, flat.shape[-1]), (((1,), (1,)), ((), ())), preferred_element_type=F32
        )
        add(2 * m, product[:rows_all])
        add(2 * m + 1, product[rows_all:])

    turn(0, even, arrive)
    if ready is not None:
        ready()
    loops = (HALF - 2) // 2

    def step(i, carry):
        m = 2 * i + 1
        turn(m, odd)
        multiply(m - 1, even)
        turn(m + 1, even)
        multiply(m, odd)
        return carry

    lax.fori_loop(0, loops, step, 0)
    now, later = even, odd
    for m in range(2 * loops, HALF):
        if m + 1 < HALF:
            turn(m + 1, later)
        multiply(m, now)
        now, later = later, now


def first_kernel(group, where, left, own, other, cos_ref, sin_ref, own_sum, other_sum, even, odd, flat):
    @pl.when(pl.program_id(0) == 0)
    def _():
        own_sum[...] = jnp.zeros_like(own_sum)
        other_sum[...] = jnp.zeros_like(other_sum)

    def add(at, product):
        own_sum[at] += product[:, : NZ * CH]
        other_sum[at] += product[:, NZ * CH :]

    for h, right in enumerate((own, other)):
        for g in range(group):
            for comp in range(2):
                flat[h * NZ : (h + 1) * NZ, :, col(g, comp)] = right[g, 0, :, comp]
    turn_and_multiply(group, where, left, cos_ref, sin_ref, even, odd, flat, add)


def second_kernel(is_own, where, landed, right, cos_ref, sin_ref, before, o0, o1, o2, o3, *refs):
    if is_own:
        mine, *refs = refs
    left, sums, even, odd, flat, left_sems, right_sems, other_sems = refs
    group = landed.shape[0]
    quarter = group // 4
    lefts = [
        pltpu.make_async_copy(
            landed.at[pl.ds(q * quarter, quarter), where[0]], left.at[pl.ds(q * quarter, quarter), 0], left_sems.at[q]
        )
        for q in range(4)
    ]
    if is_own:
        rights = [
            pltpu.make_async_copy(
                right.at[g, where[1], :, comp], flat.at[:, :, pl.ds((2 * g + comp) * FB, FB)], right_sems.at[g, comp]
            )
            for g in range(group)
            for comp in range(2)
        ]
        keep = pltpu.make_async_copy(flat, mine, other_sems.at[1])
    else:
        rights = [pltpu.make_async_copy(right.at[z], flat.at[z], right_sems.at[z, 0]) for z in range(NZ)]
    past = pltpu.make_async_copy(before, sums, other_sems.at[0])
    for copy in lefts + rights + [past]:
        copy.start()

    def arrive(g):
        if g % quarter == 0:
            lefts[g // quarter].wait()

    def ready():
        for copy in rights + [past]:
            copy.wait()
        if is_own:
            keep.start()

    def add(at, product):
        for dz, out in enumerate((o0, o1, o2, o3)):
            rows = slice(dz * CH, dz * CH + CH)
            out[at] = ((sums[at, rows] + product[rows]) * (1.0 / 128.0)).astype(BF)

    turn_and_multiply(group, where, left, cos_ref, sin_ref, even, odd, flat, add, arrive, ready)
    if is_own:
        keep.wait()


SUMS = (LAGS, NZ * CH, NZ * CH)


def spec(group, at=None):
    index_map = (lambda s, where: (s, 0, 0, 0, 0, 0)) if at is None else (lambda s, where: (s, where[at], 0, 0, 0, 0))
    return pl.BlockSpec((group, 1, NZ, 2, CH, FB), index_map)


def table_spec():
    return pl.BlockSpec((8, FB), lambda s, where: (0, 0))


def whole(shape, at=0):
    return pl.BlockSpec(shape, lambda s, where: (at, 0, 0))


def first_half(where, landed, theirs, cosine, sine):
    group = 8
    return pl.pallas_call(
        functools.partial(first_kernel, group),
        grid_spec=pltpu.PrefetchScalarGridSpec(
            num_scalar_prefetch=1,
            grid=(landed.shape[0] // group,),
            in_specs=[spec(group, 0), spec(group, 1), spec(group), table_spec(), table_spec()],
            out_specs=[whole(SUMS)] * 2,
            scratch_shapes=[
                pltpu.VMEM((2 * NZ * CH, 2 * group * FB), BF),
                pltpu.VMEM((2 * NZ * CH, 2 * group * FB), BF),
                pltpu.VMEM((2 * NZ, CH, 2 * group * FB), BF),
            ],
        ),
        out_shape=[jax.ShapeDtypeStruct(SUMS, F32)] * 2,
        compiler_params=pltpu.CompilerParams(vmem_limit_bytes=40 * 2**20),
        cost_estimate=pl.CostEstimate(flops=13 * 10**9, bytes_accessed=12 * 2**20, transcendentals=0),
        name="first_half",
    )(where, landed, landed, theirs, cosine, sine)


def second_half(where, landed, right, cosine, sine, before):
    is_own = right is None
    group = landed.shape[0]
    width = 2 * group * FB
    piece = jax.ShapeDtypeStruct((LAGS, CH, NZ * CH), BF)
    out_specs, out_shape = [whole(piece.shape)] * NZ, [piece] * NZ
    anywhere = pl.BlockSpec(memory_space=pl.ANY)
    if is_own:
        right = landed
        out_specs = out_specs + [anywhere]
        out_shape = out_shape + [jax.ShapeDtypeStruct((NZ, CH, width), BF)]
    return pl.pallas_call(
        functools.partial(second_kernel, is_own),
        grid_spec=pltpu.PrefetchScalarGridSpec(
            num_scalar_prefetch=1,
            grid=(1,),
            in_specs=[anywhere, anywhere, table_spec(), table_spec(), anywhere],
            out_specs=out_specs,
            scratch_shapes=[
                pltpu.VMEM((group, 1, NZ, 2, CH, FB), BF),
                pltpu.VMEM(SUMS, F32),
                pltpu.VMEM((2 * NZ * CH, width), BF),
                pltpu.VMEM((2 * NZ * CH, width), BF),
                pltpu.VMEM((NZ, CH, width), BF),
                pltpu.SemaphoreType.DMA((4,)),
                pltpu.SemaphoreType.DMA((group, 2)),
                pltpu.SemaphoreType.DMA((2,)),
            ],
        ),
        out_shape=out_shape,
        compiler_params=pltpu.CompilerParams(vmem_limit_bytes=40 * 2**20),
        cost_estimate=pl.CostEstimate(flops=65 * 10**8, bytes_accessed=8 * 2**20, transcendentals=0),
        name="second_half",
    )(where, landed, right, cosine, sine, before)


def total_kernel(where, *refs):
    out = refs[-1]
    width = NZ * CH
    for half in range(2):
        at = pl.multiple_of(where[half] * width, width)
        group = refs[half * NZ : (half + 1) * NZ]
        for m in range(HALF):
            for sign in range(2):
                i = 2 * m + sign
                val = group[0][i].astype(F32)
                for ref in group[1:]:
                    val = val + ref[i].astype(F32)
                lag = HALF + m if sign else (HALF - m if m else 0)
                out[0, lag, :, pl.ds(at, width)] = val


def total(where, parts):
    shape = (1, LAGS, CH, 2 * NZ * CH)
    return pl.pallas_call(
        total_kernel,
        grid_spec=pltpu.PrefetchScalarGridSpec(
            num_scalar_prefetch=1,
            grid=(1,),
            in_specs=[pl.BlockSpec(part.shape, lambda i, where: (0, 0, 0)) for part in parts],
            out_specs=pl.BlockSpec(shape, lambda i, where: (0, 0, 0, 0)),
        ),
        out_shape=jax.ShapeDtypeStruct(shape, F32),
        compiler_params=pltpu.CompilerParams(vmem_limit_bytes=32 * 2**20),
        name="total",
    )(where, *parts)


def places():
    return [
        (y, xl, c, xh, z)
        for y in range(4)
        for xl in range(2)
        for c in range(2)
        for xh in range(2)
        for z in range(NZ)
    ]


def index(y, xl, c, xh, z):
    return ((y * 2 + xl) * 2 + c) * 8 + xh * 4 + z


def body(spectra, block_pairs, band_bins):
    both = ("row", "col")
    row = lax.axis_index("row")
    col = lax.axis_index("col")
    core = row % 2
    xh = col // 4
    z = col % 4

    bins_there = lax.ppermute(
        band_bins, both, [(index(*p), index(p[0], p[1], p[2], 1 - p[3], p[4])) for p in places()]
    )
    low = jnp.where(xh == 0, band_bins, bins_there)
    high = jnp.where(xh == 0, bins_there, band_bins)
    steps = jnp.arange(8, dtype=jnp.int32)
    angle = jnp.mod(jnp.stack([low, high])[:, None, :] * steps[:, None], L).astype(F32) * (2.0 * math.pi / L)
    cosine, sine = jnp.cos(angle), jnp.sin(angle)

    where = jnp.stack([1 - core, core] + [(z + hop) % NZ for hop in HOPS]).astype(jnp.int32)
    halves = jnp.stack([1 - xh, xh]).astype(jnp.int32)

    def swap(mine):
        return lax.ppermute(
            mine, both, [(index(*p), index(p[0], p[1], 1 - p[2], p[3], p[4])) for p in places()]
        )

    def exchange(packed):
        landed = lax.all_to_all(packed.reshape(128, 2, CH, FB), both, split_axis=0, concat_axis=0, tiled=True)
        landed = landed.reshape(16, 2, NZ, 2, CH, FB)
        return landed, swap(lax.dynamic_slice_in_dim(landed, core, 1, axis=1))

    def send(parts):
        return [
            lax.ppermute(
                part,
                both,
                [(index(*p), index(p[0], p[1], p[3], 1 - p[2], (p[4] + hop) % NZ)) for p in places()],
            )
            for hop, part in zip(HOPS, parts)
        ]

    pairs, side = block_pairs.T, xh.reshape(1)
    packed0 = pack(spectra, pairs, side, 0)
    packed1 = pack(spectra, pairs, side, 1)
    packed1, cosine, sine, where, halves = lax.optimization_barrier((packed1, cosine, sine, where, halves))
    landed0, theirs0 = exchange(packed0)
    own, other = first_half(where, landed0, theirs0, cosine[0], sine[0])
    landed1 = lax.all_to_all(packed1.reshape(128, 2, CH, FB), both, split_axis=0, concat_axis=0, tiled=True)
    landed1, own, other = lax.optimization_barrier((landed1, own, other))
    landed1 = landed1.reshape(16, 2, NZ, 2, CH, FB)
    *first, mine1 = second_half(where, landed1, None, cosine[1], sine[1], own)
    theirs1 = swap(mine1)
    first = send(first)
    second = send(second_half(where, landed1, theirs1, cosine[1], sine[1], other))
    return jnp.transpose(total(halves, first + second), (0, 2, 1, 3))


def solution(mesh):
    in_specs = (P(None, "row", None, "col", None), P(), P("col"))
    out_specs = P("row", "col", None, None)
    return jax.shard_map(body, mesh=mesh, in_specs=in_specs, out_specs=out_specs, check_vma=False)
```

```python
import functools
import math

import jax
import jax.numpy as jnp
from jax import lax
from jax.experimental import pallas as pl
from jax.experimental.pallas import tpu as pltpu
from jax.sharding import PartitionSpec as P

L = 8192
LAGS = 12
HALF = LAGS // 2
EPS = 1e-06

NZ = 4
CH = 64
FB = 128
HOPS = (2, 1, 3, 0)
BF = jnp.bfloat16
F32 = jnp.float32


def pack_kernel(group, part, pairs, xh, block, out, white, sems):
    step = pl.program_id(0)
    for g in range(group):
        re = block[0, 0, g].astype(F32)
        im = block[1, 0, g].astype(F32)
        energy = jnp.mean(re * re + im * im, axis=-1, keepdims=True)
        gain = lax.rsqrt(energy + EPS)
        for comp, val in enumerate((re, im)):
            for z in range(NZ):
                at = (part * NZ + z) * FB
                white[step * group + g, z, comp] = (val[:, at : at + FB] * gain).astype(BF)

    def chosen(pair, core):
        return pairs[jnp.where(xh[0] == core, 1, 0), pair]

    def copy(pair, core):
        return pltpu.make_async_copy(
            white.at[chosen(pair, core)], out.at[pair // 2, core, pair % 2], sems.at[pair, core]
        )

    for pair in range(16):
        for core in range(2):

            @pl.when(chosen(pair, core) // group == step)
            def _(pair=pair, core=core):
                copy(pair, core).start()

    @pl.when(step == pl.num_programs(0) - 1)
    def _():
        for pair in range(16):
            for core in range(2):
                copy(pair, core).wait()


def pack(spectra, pairs, xh, part):
    blocks = spectra.shape[2]
    group = 8
    return pl.pallas_call(
        functools.partial(pack_kernel, group, part),
        grid_spec=pltpu.PrefetchScalarGridSpec(
            num_scalar_prefetch=2,
            grid=(blocks // group,),
            in_specs=[pl.BlockSpec((2, 1, group, CH, 1024), lambda p, pairs, xh: (0, 0, p, 0, 0))],
            out_specs=pl.BlockSpec(memory_space=pl.ANY),
            scratch_shapes=[
                pltpu.VMEM((blocks, NZ, 2, CH, FB), BF),
                pltpu.SemaphoreType.DMA((16, 2)),
            ],
        ),
        out_shape=jax.ShapeDtypeStruct((8, 2, 2, NZ, 2, CH, FB), BF),
        compiler_params=pltpu.CompilerParams(vmem_limit_bytes=60 * 2**20),
        cost_estimate=pl.CostEstimate(flops=16 * 2**20, bytes_accessed=8 * 2**20, transcendentals=0),
        name="pack",
    )(pairs, xh, spectra)


def col(g, comp):
    return slice((2 * g + comp) * FB, (2 * g + comp + 1) * FB)


def turn_and_multiply(group, where, left, cos_ref, sin_ref, even, odd, flat, add, arrive=None, ready=None):
    rows_all = NZ * CH

    def turn(m, turned, arrive=None):
        lag = HALF if isinstance(m, int) and m == 0 else m
        both = lag is m
        cos = jnp.broadcast_to(cos_ref[pl.ds(lag, 1), :], (CH, FB)).astype(BF)
        sin = jnp.broadcast_to(sin_ref[pl.ds(lag, 1), :], (CH, FB)).astype(BF)
        for g in range(group):
            if arrive is not None:
                arrive(g)
            for dz in range(NZ):
                z = where[2 + dz]
                re = left[g, 0, z, 0]
                im = left[g, 0, z, 1]
                rc, rs, ic, isn = re * cos, re * sin, im * cos, im * sin
                rows = slice(dz * CH, dz * CH + CH)
                more = slice(rows_all + dz * CH, rows_all + dz * CH + CH)
                turned[rows, col(g, 0)] = rc + isn
                turned[rows, col(g, 1)] = ic - rs
                turned[more, col(g, 0)] = rc - isn if both else re
                turned[more, col(g, 1)] = rs + ic if both else im

    def multiply(m, turned):
        product = lax.dot_general(
            turned[...], flat[...].reshape(-1, flat.shape[-1]), (((1,), (1,)), ((), ())), preferred_element_type=F32
        )
        add(2 * m, product[:rows_all])
        add(2 * m + 1, product[rows_all:])

    turn(0, even, arrive)
    if ready is not None:
        ready()
    loops = (HALF - 2) // 2

    def step(i, carry):
        m = 2 * i + 1
        turn(m, odd)
        multiply(m - 1, even)
        turn(m + 1, even)
        multiply(m, odd)
        return carry

    lax.fori_loop(0, loops, step, 0)
    now, later = even, odd
    for m in range(2 * loops, HALF):
        if m + 1 < HALF:
            turn(m + 1, later)
        multiply(m, now)
        now, later = later, now


def first_kernel(group, where, left, own, other, cos_ref, sin_ref, own_out, other_out, own_sum, other_sum, even, odd, flat):
    @pl.when(pl.program_id(0) == 0)
    def _():
        own_sum[...] = jnp.zeros_like(own_sum)
        other_sum[...] = jnp.zeros_like(other_sum)

    def add(at, product):
        own_sum[at] += product[:, : NZ * CH]
        other_sum[at] += product[:, NZ * CH :]

    for h, right in enumerate((own, other)):
        for g in range(group):
            for comp in range(2):
                flat[h * NZ : (h + 1) * NZ, :, col(g, comp)] = right[g, 0, :, comp]
    turn_and_multiply(group, where, left, cos_ref, sin_ref, even, odd, flat, add)

    @pl.when(pl.program_id(0) == pl.num_programs(0) - 1)
    def _():
        own_out[...] = own_sum[...].astype(BF)
        other_out[...] = other_sum[...].astype(BF)


def second_kernel(is_own, where, landed, right, cos_ref, sin_ref, before, o0, o1, o2, o3, *refs):
    if is_own:
        mine, *refs = refs
    left, sums, even, odd, flat, left_sems, right_sems, other_sems = refs
    group = landed.shape[0]
    quarter = group // 4
    lefts = [
        pltpu.make_async_copy(
            landed.at[pl.ds(q * quarter, quarter), where[0]], left.at[pl.ds(q * quarter, quarter), 0], left_sems.at[q]
        )
        for q in range(4)
    ]
    if is_own:
        rights = [
            pltpu.make_async_copy(
                right.at[g, where[1], :, comp], flat.at[:, :, pl.ds((2 * g + comp) * FB, FB)], right_sems.at[g, comp]
            )
            for g in range(group)
            for comp in range(2)
        ]
        keep = pltpu.make_async_copy(flat, mine, other_sems.at[1])
    else:
        rights = [pltpu.make_async_copy(right.at[z], flat.at[z], right_sems.at[z, 0]) for z in range(NZ)]
    past = pltpu.make_async_copy(before, sums, other_sems.at[0])
    for copy in lefts + rights + [past]:
        copy.start()

    def arrive(g):
        if g % quarter == 0:
            lefts[g // quarter].wait()

    def ready():
        for copy in rights + [past]:
            copy.wait()
        if is_own:
            keep.start()

    def add(at, product):
        for dz, out in enumerate((o0, o1, o2, o3)):
            rows = slice(dz * CH, dz * CH + CH)
            out[at] = ((sums[at, rows].astype(F32) + product[rows]) * (1.0 / 128.0)).astype(BF)

    turn_and_multiply(group, where, left, cos_ref, sin_ref, even, odd, flat, add, arrive, ready)
    if is_own:
        keep.wait()


SUMS = (LAGS, NZ * CH, NZ * CH)


def spec(group, at=None):
    index_map = (lambda s, where: (s, 0, 0, 0, 0, 0)) if at is None else (lambda s, where: (s, where[at], 0, 0, 0, 0))
    return pl.BlockSpec((group, 1, NZ, 2, CH, FB), index_map)


def table_spec():
    return pl.BlockSpec((8, FB), lambda s, where: (0, 0))


def whole(shape, at=0):
    return pl.BlockSpec(shape, lambda s, where: (at, 0, 0))


def first_half(where, landed, theirs, cosine, sine):
    group = 8
    return pl.pallas_call(
        functools.partial(first_kernel, group),
        grid_spec=pltpu.PrefetchScalarGridSpec(
            num_scalar_prefetch=1,
            grid=(landed.shape[0] // group,),
            in_specs=[spec(group, 0), spec(group, 1), spec(group), table_spec(), table_spec()],
            out_specs=[whole(SUMS)] * 2,
            scratch_shapes=[
                pltpu.VMEM(SUMS, F32),
                pltpu.VMEM(SUMS, F32),
                pltpu.VMEM((2 * NZ * CH, 2 * group * FB), BF),
                pltpu.VMEM((2 * NZ * CH, 2 * group * FB), BF),
                pltpu.VMEM((2 * NZ, CH, 2 * group * FB), BF),
            ],
        ),
        out_shape=[jax.ShapeDtypeStruct(SUMS, BF)] * 2,
        compiler_params=pltpu.CompilerParams(vmem_limit_bytes=40 * 2**20),
        cost_estimate=pl.CostEstimate(flops=13 * 10**9, bytes_accessed=12 * 2**20, transcendentals=0),
        name="first_half",
    )(where, landed, landed, theirs, cosine, sine)


def second_half(where, landed, right, cosine, sine, before):
    is_own = right is None
    group = landed.shape[0]
    width = 2 * group * FB
    piece = jax.ShapeDtypeStruct((LAGS, CH, NZ * CH), BF)
    out_specs, out_shape = [whole(piece.shape)] * NZ, [piece] * NZ
    anywhere = pl.BlockSpec(memory_space=pl.ANY)
    if is_own:
        right = landed
        out_specs = out_specs + [anywhere]
        out_shape = out_shape + [jax.ShapeDtypeStruct((NZ, CH, width), BF)]
    return pl.pallas_call(
        functools.partial(second_kernel, is_own),
        grid_spec=pltpu.PrefetchScalarGridSpec(
            num_scalar_prefetch=1,
            grid=(1,),
            in_specs=[anywhere, anywhere, table_spec(), table_spec(), anywhere],
            out_specs=out_specs,
            scratch_shapes=[
                pltpu.VMEM((group, 1, NZ, 2, CH, FB), BF),
                pltpu.VMEM(SUMS, BF),
                pltpu.VMEM((2 * NZ * CH, width), BF),
                pltpu.VMEM((2 * NZ * CH, width), BF),
                pltpu.VMEM((NZ, CH, width), BF),
                pltpu.SemaphoreType.DMA((4,)),
                pltpu.SemaphoreType.DMA((group, 2)),
                pltpu.SemaphoreType.DMA((2,)),
            ],
        ),
        out_shape=out_shape,
        compiler_params=pltpu.CompilerParams(vmem_limit_bytes=40 * 2**20),
        cost_estimate=pl.CostEstimate(flops=65 * 10**8, bytes_accessed=8 * 2**20, transcendentals=0),
        name="second_half",
    )(where, landed, right, cosine, sine, before)


def total_kernel(where, *refs):
    out = refs[-1]
    group = refs[:NZ]
    for m in range(HALF):
        for sign in range(2):
            i = 2 * m + sign
            val = group[0][i].astype(F32)
            for ref in group[1:]:
                val = val + ref[i].astype(F32)
            lag = HALF + m if sign else (HALF - m if m else 0)
            out[0, lag] = val


def total(where, half, parts, filled=None):
    shape = (1, LAGS, CH, 2 * NZ * CH)
    given = [] if filled is None else [filled]
    return pl.pallas_call(
        total_kernel,
        grid_spec=pltpu.PrefetchScalarGridSpec(
            num_scalar_prefetch=1,
            grid=(1,),
            in_specs=[pl.BlockSpec(part.shape, lambda i, where: (0, 0, 0)) for part in parts]
            + [pl.BlockSpec(memory_space=pl.ANY)] * len(given),
            out_specs=pl.BlockSpec((1, LAGS, CH, NZ * CH), lambda i, where: (0, 0, 0, where[half])),
        ),
        out_shape=jax.ShapeDtypeStruct(shape, F32),
        input_output_aliases={1 + len(parts): 0} if given else {},
        compiler_params=pltpu.CompilerParams(vmem_limit_bytes=32 * 2**20),
        name="total",
    )(where, *parts, *given)


def places():
    return [
        (y, xl, c, xh, z)
        for y in range(4)
        for xl in range(2)
        for c in range(2)
        for xh in range(2)
        for z in range(NZ)
    ]


def index(y, xl, c, xh, z):
    return ((y * 2 + xl) * 2 + c) * 8 + xh * 4 + z


def body(spectra, block_pairs, band_bins):
    both = ("row", "col")
    row = lax.axis_index("row")
    col = lax.axis_index("col")
    core = row % 2
    xh = col // 4
    z = col % 4

    bins_there = lax.ppermute(
        band_bins, both, [(index(*p), index(p[0], p[1], p[2], 1 - p[3], p[4])) for p in places()]
    )
    low = jnp.where(xh == 0, band_bins, bins_there)
    high = jnp.where(xh == 0, bins_there, band_bins)
    steps = jnp.arange(8, dtype=jnp.int32)
    angle = jnp.mod(jnp.stack([low, high])[:, None, :] * steps[:, None], L).astype(F32) * (2.0 * math.pi / L)
    cosine, sine = jnp.cos(angle), jnp.sin(angle)

    where = jnp.stack([1 - core, core] + [(z + hop) % NZ for hop in HOPS]).astype(jnp.int32)
    halves = jnp.stack([1 - xh, xh]).astype(jnp.int32)

    def swap(mine):
        return lax.ppermute(
            mine, both, [(index(*p), index(p[0], p[1], 1 - p[2], p[3], p[4])) for p in places()]
        )

    def exchange(packed):
        landed = lax.all_to_all(packed.reshape(128, 2, CH, FB), both, split_axis=0, concat_axis=0, tiled=True)
        landed = landed.reshape(16, 2, NZ, 2, CH, FB)
        return landed, swap(lax.dynamic_slice_in_dim(landed, core, 1, axis=1))

    def send(parts):
        return [
            lax.ppermute(
                part,
                both,
                [(index(*p), index(p[0], p[1], p[3], 1 - p[2], (p[4] + hop) % NZ)) for p in places()],
            )
            for hop, part in zip(HOPS, parts)
        ]

    pairs, side = block_pairs.T, xh.reshape(1)
    packed0 = pack(spectra, pairs, side, 0)
    packed1 = pack(spectra, pairs, side, 1)
    packed1, cosine, sine, where, halves = lax.optimization_barrier((packed1, cosine, sine, where, halves))
    landed0, theirs0 = exchange(packed0)
    own, other = first_half(where, landed0, theirs0, cosine[0], sine[0])
    landed1 = lax.all_to_all(packed1.reshape(128, 2, CH, FB), both, split_axis=0, concat_axis=0, tiled=True)
    landed1, own, other = lax.optimization_barrier((landed1, own, other))
    landed1 = landed1.reshape(16, 2, NZ, 2, CH, FB)
    *first, mine1 = second_half(where, landed1, None, cosine[1], sine[1], own)
    theirs1 = swap(mine1)
    first = send(first)
    second = send(second_half(where, landed1, theirs1, cosine[1], sine[1], other))
    filled = total(halves, 1, second, total(halves, 0, first))
    return jnp.transpose(filled, (0, 2, 1, 3))


def solution(mesh):
    in_specs = (P(None, "row", None, "col", None), P(), P("col"))
    out_specs = P("row", "col", None, None)
    return jax.shard_map(body, mesh=mesh, in_specs=in_specs, out_specs=out_specs, check_vma=False)
```

```python
import functools
import math

import jax
import jax.numpy as jnp
from jax import lax
from jax.experimental import pallas as pl
from jax.experimental.pallas import tpu as pltpu
from jax.sharding import PartitionSpec as P

L = 8192
LAGS = 12
HALF = LAGS // 2
EPS = 1e-06

NZ = 4
CH = 64
FB = 128
HOPS = (2, 0, 1, 3)
BF = jnp.bfloat16
F32 = jnp.float32


def pack_kernel(group, part, pairs, xh, block, out, white, sems):
    step = pl.program_id(0)
    for g in range(group):
        re = block[0, 0, g].astype(F32)
        im = block[1, 0, g].astype(F32)
        energy = jnp.mean(re * re + im * im, axis=-1, keepdims=True)
        gain = lax.rsqrt(energy + EPS)
        for comp, val in enumerate((re, im)):
            for z in range(NZ):
                at = (part * NZ + z) * FB
                white[step * group + g, z, comp] = (val[:, at : at + FB] * gain).astype(BF)

    def chosen(pair, core):
        return pairs[jnp.where(xh[0] == core, 1, 0), pair]

    def copy(pair, core):
        return pltpu.make_async_copy(
            white.at[chosen(pair, core)], out.at[pair // 2, core, pair % 2], sems.at[pair, core]
        )

    for pair in range(16):
        for core in range(2):

            @pl.when(chosen(pair, core) // group == step)
            def _(pair=pair, core=core):
                copy(pair, core).start()

    @pl.when(step == pl.num_programs(0) - 1)
    def _():
        for pair in range(16):
            for core in range(2):
                copy(pair, core).wait()


def pack(spectra, pairs, xh, part):
    blocks = spectra.shape[2]
    group = 8
    return pl.pallas_call(
        functools.partial(pack_kernel, group, part),
        grid_spec=pltpu.PrefetchScalarGridSpec(
            num_scalar_prefetch=2,
            grid=(blocks // group,),
            in_specs=[pl.BlockSpec((2, 1, group, CH, 1024), lambda p, pairs, xh: (0, 0, p, 0, 0))],
            out_specs=pl.BlockSpec(memory_space=pl.ANY),
            scratch_shapes=[
                pltpu.VMEM((blocks, NZ, 2, CH, FB), BF),
                pltpu.SemaphoreType.DMA((16, 2)),
            ],
        ),
        out_shape=jax.ShapeDtypeStruct((8, 2, 2, NZ, 2, CH, FB), BF),
        compiler_params=pltpu.CompilerParams(vmem_limit_bytes=60 * 2**20),
        cost_estimate=pl.CostEstimate(flops=16 * 2**20, bytes_accessed=8 * 2**20, transcendentals=0),
        name="pack",
    )(pairs, xh, spectra)


def col(g, comp):
    return slice((2 * g + comp) * FB, (2 * g + comp + 1) * FB)


def turn_and_multiply(group, slots, get, cos_ref, sin_ref, even, odd, flat, add, arrive=None, ready=None):
    rows_all = slots * CH

    def turn(m, turned, arrive=None):
        lag = HALF if isinstance(m, int) and m == 0 else m
        both = lag is m
        cos = jnp.broadcast_to(cos_ref[pl.ds(lag, 1), :], (CH, FB)).astype(BF)
        sin = jnp.broadcast_to(sin_ref[pl.ds(lag, 1), :], (CH, FB)).astype(BF)
        for g in range(group):
            if arrive is not None:
                arrive(g)
            for dz in range(slots):
                re = get(g, dz, 0)
                im = get(g, dz, 1)
                rc, rs, ic, isn = re * cos, re * sin, im * cos, im * sin
                rows = slice(dz * CH, dz * CH + CH)
                more = slice(rows_all + dz * CH, rows_all + dz * CH + CH)
                turned[rows, col(g, 0)] = rc + isn
                turned[rows, col(g, 1)] = ic - rs
                turned[more, col(g, 0)] = rc - isn if both else re
                turned[more, col(g, 1)] = rs + ic if both else im

    def multiply(m, turned):
        product = lax.dot_general(
            turned[...], flat[...].reshape(-1, flat.shape[-1]), (((1,), (1,)), ((), ())), preferred_element_type=F32
        )
        add(2 * m, product[:rows_all])
        add(2 * m + 1, product[rows_all:])

    turn(0, even, arrive)
    if ready is not None:
        ready()
    loops = (HALF - 2) // 2

    def step(i, carry):
        m = 2 * i + 1
        turn(m, odd)
        multiply(m - 1, even)
        turn(m + 1, even)
        multiply(m, odd)
        return carry

    lax.fori_loop(0, loops, step, 0)
    now, later = even, odd
    for m in range(2 * loops, HALF):
        if m + 1 < HALF:
            turn(m + 1, later)
        multiply(m, now)
        now, later = later, now


def first_kernel(group, where, left, own, other, cos_ref, sin_ref, own_out, other_out, own_sum, other_sum, even, odd, flat):
    @pl.when(pl.program_id(0) == 0)
    def _():
        own_sum[...] = jnp.zeros_like(own_sum)
        other_sum[...] = jnp.zeros_like(other_sum)

    def add(at, product):
        own_sum[at] += product[:, : NZ * CH]
        other_sum[at] += product[:, NZ * CH :]

    for h, right in enumerate((own, other)):
        for g in range(group):
            for comp in range(2):
                flat[h * NZ : (h + 1) * NZ, :, col(g, comp)] = right[g, 0, :, comp]

    def get(g, dz, comp):
        return left[g, 0, where[2 + dz], comp]

    turn_and_multiply(group, NZ, get, cos_ref, sin_ref, even, odd, flat, add)

    @pl.when(pl.program_id(0) == pl.num_programs(0) - 1)
    def _():
        own_out[...] = own_sum[...].astype(BF)
        other_out[...] = other_sum[...].astype(BF)


def second_kernel(is_own, start, count, where, landed, right, cos_ref, sin_ref, before, *refs):
    outs, refs = refs[:count], refs[count:]
    if is_own:
        mine, *refs = refs
    left, sums, even, odd, flat, left_sems, right_sems, other_sems = refs
    group = landed.shape[0]
    quarter = group // 4
    lefts = [
        [
            pltpu.make_async_copy(
                landed.at[pl.ds(q * quarter, quarter), where[0], where[2 + start + k]],
                left.at[k, pl.ds(q * quarter, quarter)],
                left_sems.at[q, k],
            )
            for k in range(count)
        ]
        for q in range(4)
    ]
    if is_own:
        rights = [
            pltpu.make_async_copy(
                right.at[g, where[1], :, comp], flat.at[:, :, pl.ds((2 * g + comp) * FB, FB)], right_sems.at[g, comp]
            )
            for g in range(group)
            for comp in range(2)
        ]
        keep = pltpu.make_async_copy(flat, mine, other_sems.at[1])
    else:
        rights = [pltpu.make_async_copy(right.at[z], flat.at[z], right_sems.at[z, 0]) for z in range(NZ)]
    past = pltpu.make_async_copy(before.at[:, pl.ds(start * CH, count * CH)], sums, other_sems.at[0])
    for copy in sum(lefts, []) + rights + [past]:
        copy.start()

    def get(g, dz, comp):
        return left[dz, g, comp]

    def arrive(g):
        if g % quarter == 0:
            for copy in lefts[g // quarter]:
                copy.wait()

    def ready():
        for copy in rights + [past]:
            copy.wait()
        if is_own:
            keep.start()

    def add(at, product):
        for k, out in enumerate(outs):
            rows = slice(k * CH, k * CH + CH)
            out[at] = ((sums[at, rows].astype(F32) + product[rows]) * (1.0 / 128.0)).astype(BF)

    turn_and_multiply(group, count, get, cos_ref, sin_ref, even, odd, flat, add, arrive, ready)
    if is_own:
        keep.wait()


SUMS = (LAGS, NZ * CH, NZ * CH)


def spec(group, at=None):
    index_map = (lambda s, where: (s, 0, 0, 0, 0, 0)) if at is None else (lambda s, where: (s, where[at], 0, 0, 0, 0))
    return pl.BlockSpec((group, 1, NZ, 2, CH, FB), index_map)


def table_spec():
    return pl.BlockSpec((8, FB), lambda s, where: (0, 0))


def whole(shape, at=0):
    return pl.BlockSpec(shape, lambda s, where: (at, 0, 0))


def first_half(where, landed, theirs, cosine, sine):
    group = 8
    return pl.pallas_call(
        functools.partial(first_kernel, group),
        grid_spec=pltpu.PrefetchScalarGridSpec(
            num_scalar_prefetch=1,
            grid=(landed.shape[0] // group,),
            in_specs=[spec(group, 0), spec(group, 1), spec(group), table_spec(), table_spec()],
            out_specs=[whole(SUMS)] * 2,
            scratch_shapes=[
                pltpu.VMEM(SUMS, F32),
                pltpu.VMEM(SUMS, F32),
                pltpu.VMEM((2 * NZ * CH, 2 * group * FB), BF),
                pltpu.VMEM((2 * NZ * CH, 2 * group * FB), BF),
                pltpu.VMEM((2 * NZ, CH, 2 * group * FB), BF),
            ],
        ),
        out_shape=[jax.ShapeDtypeStruct(SUMS, BF)] * 2,
        compiler_params=pltpu.CompilerParams(vmem_limit_bytes=40 * 2**20),
        cost_estimate=pl.CostEstimate(flops=13 * 10**9, bytes_accessed=12 * 2**20, transcendentals=0),
        name="first_half",
    )(where, landed, landed, theirs, cosine, sine)


def second_half(where, landed, right, cosine, sine, before, start, count):
    is_own = right is None
    group = landed.shape[0]
    width = 2 * group * FB
    piece = jax.ShapeDtypeStruct((LAGS, CH, NZ * CH), BF)
    out_specs, out_shape = [whole(piece.shape)] * count, [piece] * count
    anywhere = pl.BlockSpec(memory_space=pl.ANY)
    if is_own:
        right = landed
        out_specs = out_specs + [anywhere]
        out_shape = out_shape + [jax.ShapeDtypeStruct((NZ, CH, width), BF)]
    return pl.pallas_call(
        functools.partial(second_kernel, is_own, start, count),
        grid_spec=pltpu.PrefetchScalarGridSpec(
            num_scalar_prefetch=1,
            grid=(1,),
            in_specs=[anywhere, anywhere, table_spec(), table_spec(), anywhere],
            out_specs=out_specs,
            scratch_shapes=[
                pltpu.VMEM((count, group, 2, CH, FB), BF),
                pltpu.VMEM((LAGS, count * CH, NZ * CH), BF),
                pltpu.VMEM((2 * count * CH, width), BF),
                pltpu.VMEM((2 * count * CH, width), BF),
                pltpu.VMEM((NZ, CH, width), BF),
                pltpu.SemaphoreType.DMA((4, count)),
                pltpu.SemaphoreType.DMA((group, 2)),
                pltpu.SemaphoreType.DMA((2,)),
            ],
        ),
        out_shape=out_shape,
        compiler_params=pltpu.CompilerParams(vmem_limit_bytes=40 * 2**20),
        cost_estimate=pl.CostEstimate(flops=10**8, bytes_accessed=2**20, transcendentals=0),
        name="second_half",
    )(where, landed, right, cosine, sine, before)


def total_kernel(where, *refs):
    out = refs[-1]
    group = refs[:NZ]
    for m in range(HALF):
        for sign in range(2):
            i = 2 * m + sign
            val = group[0][i].astype(F32)
            for ref in group[1:]:
                val = val + ref[i].astype(F32)
            lag = HALF + m if sign else (HALF - m if m else 0)
            out[0, lag] = val


def total(where, half, parts, filled=None):
    shape = (1, LAGS, CH, 2 * NZ * CH)
    given = [] if filled is None else [filled]
    return pl.pallas_call(
        total_kernel,
        grid_spec=pltpu.PrefetchScalarGridSpec(
            num_scalar_prefetch=1,
            grid=(1,),
            in_specs=[pl.BlockSpec(part.shape, lambda i, where: (0, 0, 0)) for part in parts]
            + [pl.BlockSpec(memory_space=pl.ANY)] * len(given),
            out_specs=pl.BlockSpec((1, LAGS, CH, NZ * CH), lambda i, where: (0, 0, 0, where[half])),
        ),
        out_shape=jax.ShapeDtypeStruct(shape, F32),
        input_output_aliases={1 + len(parts): 0} if given else {},
        compiler_params=pltpu.CompilerParams(vmem_limit_bytes=32 * 2**20),
        name="total",
    )(where, *parts, *given)


def places():
    return [
        (y, xl, c, xh, z)
        for y in range(4)
        for xl in range(2)
        for c in range(2)
        for xh in range(2)
        for z in range(NZ)
    ]


def index(y, xl, c, xh, z):
    return ((y * 2 + xl) * 2 + c) * 8 + xh * 4 + z


def body(spectra, block_pairs, band_bins):
    both = ("row", "col")
    row = lax.axis_index("row")
    col = lax.axis_index("col")
    core = row % 2
    xh = col // 4
    z = col % 4

    bins_there = lax.ppermute(
        band_bins, both, [(index(*p), index(p[0], p[1], p[2], 1 - p[3], p[4])) for p in places()]
    )
    low = jnp.where(xh == 0, band_bins, bins_there)
    high = jnp.where(xh == 0, bins_there, band_bins)
    steps = jnp.arange(8, dtype=jnp.int32)
    angle = jnp.mod(jnp.stack([low, high])[:, None, :] * steps[:, None], L).astype(F32) * (2.0 * math.pi / L)
    cosine, sine = jnp.cos(angle), jnp.sin(angle)

    where = jnp.stack([1 - core, core] + [(z + hop) % NZ for hop in HOPS]).astype(jnp.int32)
    halves = jnp.stack([1 - xh, xh]).astype(jnp.int32)

    def swap(mine):
        return lax.ppermute(
            mine, both, [(index(*p), index(p[0], p[1], 1 - p[2], p[3], p[4])) for p in places()]
        )

    def exchange(packed):
        landed = lax.all_to_all(packed.reshape(128, 2, CH, FB), both, split_axis=0, concat_axis=0, tiled=True)
        landed = landed.reshape(16, 2, NZ, 2, CH, FB)
        return landed, swap(lax.dynamic_slice_in_dim(landed, core, 1, axis=1))

    def send(parts, start):
        return [
            lax.ppermute(
                part,
                both,
                [(index(*p), index(p[0], p[1], p[3], 1 - p[2], (p[4] + hop) % NZ)) for p in places()],
            )
            for hop, part in zip(HOPS[start:], parts)
        ]

    pairs, side = block_pairs.T, xh.reshape(1)
    packed0 = pack(spectra, pairs, side, 0)
    packed1 = pack(spectra, pairs, side, 1)
    packed1, cosine, sine, where, halves = lax.optimization_barrier((packed1, cosine, sine, where, halves))
    landed0, theirs0 = exchange(packed0)
    own, other = first_half(where, landed0, theirs0, cosine[0], sine[0])
    landed1 = lax.all_to_all(packed1.reshape(128, 2, CH, FB), both, split_axis=0, concat_axis=0, tiled=True)
    landed1, own, other = lax.optimization_barrier((landed1, own, other))
    landed1 = landed1.reshape(16, 2, NZ, 2, CH, FB)
    def chunk(right, before, start, count):
        return second_half(where, landed1, right, cosine[1], sine[1], before, start, count)

    *pieces, mine1 = chunk(None, own, 0, NZ)
    theirs1 = swap(mine1)
    early = chunk(theirs1, other, 0, 2)
    theirs1, _ = lax.optimization_barrier((theirs1, early[0]))
    late = chunk(theirs1, other, 2, 2)
    first = send(pieces, 0)
    second = send(early, 0) + send(late, 2)
    filled = total(halves, 1, second, total(halves, 0, first))
    return jnp.transpose(filled, (0, 2, 1, 3))


def solution(mesh):
    in_specs = (P(None, "row", None, "col", None), P(), P("col"))
    out_specs = P("row", "col", None, None)
    return jax.shard_map(body, mesh=mesh, in_specs=in_specs, out_specs=out_specs, check_vma=False)
```

```python
import functools
import math

import jax
import jax.numpy as jnp
from jax import lax
from jax.experimental import pallas as pl
from jax.experimental.pallas import tpu as pltpu
from jax.sharding import PartitionSpec as P

L = 8192
LAGS = 12
HALF = LAGS // 2
EPS = 1e-06

NZ = 4
CH = 64
FB = 128
HOPS = (2, 1, 3, 0)
BF = jnp.bfloat16
F32 = jnp.float32


def pack_kernel(group, part, pairs, xh, block, out, white, sems):
    step = pl.program_id(0)
    for g in range(group):
        re = block[0, 0, g].astype(F32)
        im = block[1, 0, g].astype(F32)
        energy = jnp.mean(re * re + im * im, axis=-1, keepdims=True)
        gain = lax.rsqrt(energy + EPS)
        for comp, val in enumerate((re, im)):
            for z in range(NZ):
                at = (part * NZ + z) * FB
                white[step * group + g, z, comp] = (val[:, at : at + FB] * gain).astype(BF)

    def chosen(pair, core):
        return pairs[jnp.where(xh[0] == core, 1, 0), pair]

    def copy(pair, core):
        return pltpu.make_async_copy(
            white.at[chosen(pair, core)], out.at[pair // 2, core, pair % 2], sems.at[pair, core]
        )

    for pair in range(16):
        for core in range(2):

            @pl.when(chosen(pair, core) // group == step)
            def _(pair=pair, core=core):
                copy(pair, core).start()

    @pl.when(step == pl.num_programs(0) - 1)
    def _():
        for pair in range(16):
            for core in range(2):
                copy(pair, core).wait()


def pack(spectra, pairs, xh, part):
    blocks = spectra.shape[2]
    group = 8
    return pl.pallas_call(
        functools.partial(pack_kernel, group, part),
        grid_spec=pltpu.PrefetchScalarGridSpec(
            num_scalar_prefetch=2,
            grid=(blocks // group,),
            in_specs=[pl.BlockSpec((2, 1, group, CH, 1024), lambda p, pairs, xh: (0, 0, p, 0, 0))],
            out_specs=pl.BlockSpec(memory_space=pl.ANY),
            scratch_shapes=[
                pltpu.VMEM((blocks, NZ, 2, CH, FB), BF),
                pltpu.SemaphoreType.DMA((16, 2)),
            ],
        ),
        out_shape=jax.ShapeDtypeStruct((8, 2, 2, NZ, 2, CH, FB), BF),
        compiler_params=pltpu.CompilerParams(vmem_limit_bytes=60 * 2**20),
        cost_estimate=pl.CostEstimate(flops=16 * 2**20, bytes_accessed=8 * 2**20, transcendentals=0),
        name="pack",
    )(pairs, xh, spectra)


def col(g, comp):
    return slice((2 * g + comp) * FB, (2 * g + comp + 1) * FB)


def turn_and_multiply(group, slots, get, cos_ref, sin_ref, even, odd, flat, add, arrive=None, ready=None):
    rows_all = slots * CH

    def turn(m, turned, arrive=None):
        lag = HALF if isinstance(m, int) and m == 0 else m
        both = lag is m
        cos = jnp.broadcast_to(cos_ref[pl.ds(lag, 1), :], (CH, FB)).astype(BF)
        sin = jnp.broadcast_to(sin_ref[pl.ds(lag, 1), :], (CH, FB)).astype(BF)
        for g in range(group):
            if arrive is not None:
                arrive(g)
            for dz in range(slots):
                re = get(g, dz, 0)
                im = get(g, dz, 1)
                rc, rs, ic, isn = re * cos, re * sin, im * cos, im * sin
                rows = slice(dz * CH, dz * CH + CH)
                more = slice(rows_all + dz * CH, rows_all + dz * CH + CH)
                turned[rows, col(g, 0)] = rc + isn
                turned[rows, col(g, 1)] = ic - rs
                turned[more, col(g, 0)] = rc - isn if both else re
                turned[more, col(g, 1)] = rs + ic if both else im

    def multiply(m, turned):
        product = lax.dot_general(
            turned[...], flat[...].reshape(-1, flat.shape[-1]), (((1,), (1,)), ((), ())), preferred_element_type=F32
        )
        add(2 * m, product[:rows_all])
        add(2 * m + 1, product[rows_all:])

    turn(0, even, arrive)
    if ready is not None:
        ready()
    loops = (HALF - 2) // 2

    def step(i, carry):
        m = 2 * i + 1
        turn(m, odd)
        multiply(m - 1, even)
        turn(m + 1, even)
        multiply(m, odd)
        return carry

    lax.fori_loop(0, loops, step, 0)
    now, later = even, odd
    for m in range(2 * loops, HALF):
        if m + 1 < HALF:
            turn(m + 1, later)
        multiply(m, now)
        now, later = later, now


def first_kernel(group, where, left, own, other, cos_ref, sin_ref, own_out, other_out, own_sum, other_sum, even, odd, flat):
    @pl.when(pl.program_id(0) == 0)
    def _():
        own_sum[...] = jnp.zeros_like(own_sum)
        other_sum[...] = jnp.zeros_like(other_sum)

    def add(at, product):
        own_sum[at] += product[:, : NZ * CH]
        other_sum[at] += product[:, NZ * CH :]

    for h, right in enumerate((own, other)):
        for g in range(group):
            for comp in range(2):
                flat[h * NZ : (h + 1) * NZ, :, col(g, comp)] = right[g, 0, :, comp]

    def get(g, dz, comp):
        return left[g, 0, where[2 + dz], comp]

    turn_and_multiply(group, NZ, get, cos_ref, sin_ref, even, odd, flat, add)

    @pl.when(pl.program_id(0) == pl.num_programs(0) - 1)
    def _():
        own_out[...] = own_sum[...].astype(BF)
        other_out[...] = other_sum[...].astype(BF)


def second_kernel(is_own, start, count, where, landed, right, cos_ref, sin_ref, before, *refs):
    outs, refs = refs[:count], refs[count:]
    if is_own:
        mine, *refs = refs
    left, sums, even, odd, flat, left_sems, right_sems, other_sems = refs
    group = landed.shape[0]
    quarter = group // 4
    lefts = [
        [
            pltpu.make_async_copy(
                landed.at[pl.ds(q * quarter, quarter), where[0], where[2 + start + k]],
                left.at[k, pl.ds(q * quarter, quarter)],
                left_sems.at[q, k],
            )
            for k in range(count)
        ]
        for q in range(4)
    ]
    if is_own:
        rights = [
            pltpu.make_async_copy(
                right.at[g, where[1], :, comp], flat.at[:, :, pl.ds((2 * g + comp) * FB, FB)], right_sems.at[g, comp]
            )
            for g in range(group)
            for comp in range(2)
        ]
        keep = pltpu.make_async_copy(flat, mine, other_sems.at[1])
    else:
        rights = [pltpu.make_async_copy(right.at[z], flat.at[z], right_sems.at[z, 0]) for z in range(NZ)]
    past = pltpu.make_async_copy(before.at[:, pl.ds(start * CH, count * CH)], sums, other_sems.at[0])
    for copy in sum(lefts, []) + rights + [past]:
        copy.start()

    def get(g, dz, comp):
        return left[dz, g, comp]

    def arrive(g):
        if g % quarter == 0:
            for copy in lefts[g // quarter]:
                copy.wait()

    def ready():
        for copy in rights + [past]:
            copy.wait()
        if is_own:
            keep.start()

    def add(at, product):
        for k, out in enumerate(outs):
            rows = slice(k * CH, k * CH + CH)
            out[at] = ((sums[at, rows].astype(F32) + product[rows]) * (1.0 / 128.0)).astype(BF)

    turn_and_multiply(group, count, get, cos_ref, sin_ref, even, odd, flat, add, arrive, ready)
    if is_own:
        keep.wait()


SUMS = (LAGS, NZ * CH, NZ * CH)


def spec(group, at=None):
    index_map = (lambda s, where: (s, 0, 0, 0, 0, 0)) if at is None else (lambda s, where: (s, where[at], 0, 0, 0, 0))
    return pl.BlockSpec((group, 1, NZ, 2, CH, FB), index_map)


def table_spec():
    return pl.BlockSpec((8, FB), lambda s, where: (0, 0))


def whole(shape, at=0):
    return pl.BlockSpec(shape, lambda s, where: (at, 0, 0))


def first_half(where, landed, theirs, cosine, sine):
    group = 8
    return pl.pallas_call(
        functools.partial(first_kernel, group),
        grid_spec=pltpu.PrefetchScalarGridSpec(
            num_scalar_prefetch=1,
            grid=(landed.shape[0] // group,),
            in_specs=[spec(group, 0), spec(group, 1), spec(group), table_spec(), table_spec()],
            out_specs=[whole(SUMS)] * 2,
            scratch_shapes=[
                pltpu.VMEM(SUMS, F32),
                pltpu.VMEM(SUMS, F32),
                pltpu.VMEM((2 * NZ * CH, 2 * group * FB), BF),
                pltpu.VMEM((2 * NZ * CH, 2 * group * FB), BF),
                pltpu.VMEM((2 * NZ, CH, 2 * group * FB), BF),
            ],
        ),
        out_shape=[jax.ShapeDtypeStruct(SUMS, BF)] * 2,
        compiler_params=pltpu.CompilerParams(vmem_limit_bytes=40 * 2**20),
        cost_estimate=pl.CostEstimate(flops=13 * 10**9, bytes_accessed=12 * 2**20, transcendentals=0),
        name="first_half",
    )(where, landed, landed, theirs, cosine, sine)


def second_half(where, landed, right, cosine, sine, before, start, count):
    is_own = right is None
    group = landed.shape[0]
    width = 2 * group * FB
    piece = jax.ShapeDtypeStruct((LAGS, CH, NZ * CH), BF)
    out_specs, out_shape = [whole(piece.shape)] * count, [piece] * count
    anywhere = pl.BlockSpec(memory_space=pl.ANY)
    if is_own:
        right = landed
        out_specs = out_specs + [anywhere]
        out_shape = out_shape + [jax.ShapeDtypeStruct((NZ, CH, width), BF)]
    return pl.pallas_call(
        functools.partial(second_kernel, is_own, start, count),
        grid_spec=pltpu.PrefetchScalarGridSpec(
            num_scalar_prefetch=1,
            grid=(1,),
            in_specs=[anywhere, anywhere, table_spec(), table_spec(), anywhere],
            out_specs=out_specs,
            scratch_shapes=[
                pltpu.VMEM((count, group, 2, CH, FB), BF),
                pltpu.VMEM((LAGS, count * CH, NZ * CH), BF),
                pltpu.VMEM((2 * count * CH, width), BF),
                pltpu.VMEM((2 * count * CH, width), BF),
                pltpu.VMEM((NZ, CH, width), BF),
                pltpu.SemaphoreType.DMA((4, count)),
                pltpu.SemaphoreType.DMA((group, 2)),
                pltpu.SemaphoreType.DMA((2,)),
            ],
        ),
        out_shape=out_shape,
        compiler_params=pltpu.CompilerParams(vmem_limit_bytes=40 * 2**20),
        cost_estimate=pl.CostEstimate(flops=10**8, bytes_accessed=2**20, transcendentals=0),
        name="second_half",
    )(where, landed, right, cosine, sine, before)


def total_kernel(where, *refs):
    out = refs[-1]
    group = refs[:NZ]
    for m in range(HALF):
        for sign in range(2):
            i = 2 * m + sign
            val = group[0][i].astype(F32)
            for ref in group[1:]:
                val = val + ref[i].astype(F32)
            lag = HALF + m if sign else (HALF - m if m else 0)
            out[0, lag] = val


def total(where, half, parts, filled=None):
    shape = (1, LAGS, CH, 2 * NZ * CH)
    given = [] if filled is None else [filled]
    return pl.pallas_call(
        total_kernel,
        grid_spec=pltpu.PrefetchScalarGridSpec(
            num_scalar_prefetch=1,
            grid=(1,),
            in_specs=[pl.BlockSpec(part.shape, lambda i, where: (0, 0, 0)) for part in parts]
            + [pl.BlockSpec(memory_space=pl.ANY)] * len(given),
            out_specs=pl.BlockSpec((1, LAGS, CH, NZ * CH), lambda i, where: (0, 0, 0, where[half])),
        ),
        out_shape=jax.ShapeDtypeStruct(shape, F32),
        input_output_aliases={1 + len(parts): 0} if given else {},
        compiler_params=pltpu.CompilerParams(vmem_limit_bytes=32 * 2**20),
        name="total",
    )(where, *parts, *given)


def places():
    return [
        (y, xl, c, xh, z)
        for y in range(4)
        for xl in range(2)
        for c in range(2)
        for xh in range(2)
        for z in range(NZ)
    ]


def index(y, xl, c, xh, z):
    return ((y * 2 + xl) * 2 + c) * 8 + xh * 4 + z


def body(spectra, block_pairs, band_bins):
    both = ("row", "col")
    row = lax.axis_index("row")
    col = lax.axis_index("col")
    core = row % 2
    xh = col // 4
    z = col % 4

    bins_there = lax.ppermute(
        band_bins, both, [(index(*p), index(p[0], p[1], p[2], 1 - p[3], p[4])) for p in places()]
    )
    low = jnp.where(xh == 0, band_bins, bins_there)
    high = jnp.where(xh == 0, bins_there, band_bins)
    steps = jnp.arange(8, dtype=jnp.int32)
    angle = jnp.mod(jnp.stack([low, high])[:, None, :] * steps[:, None], L).astype(F32) * (2.0 * math.pi / L)
    cosine, sine = jnp.cos(angle), jnp.sin(angle)

    where = jnp.stack([1 - core, core] + [(z + hop) % NZ for hop in HOPS]).astype(jnp.int32)
    halves = jnp.stack([1 - xh, xh]).astype(jnp.int32)

    def swap(mine):
        return lax.ppermute(
            mine, both, [(index(*p), index(p[0], p[1], 1 - p[2], p[3], p[4])) for p in places()]
        )

    def exchange(packed):
        landed = lax.all_to_all(packed.reshape(128, 2, CH, FB), both, split_axis=0, concat_axis=0, tiled=True)
        landed = landed.reshape(16, 2, NZ, 2, CH, FB)
        return landed, swap(lax.dynamic_slice_in_dim(landed, core, 1, axis=1))

    def send(parts, start):
        return [
            lax.ppermute(
                part,
                both,
                [(index(*p), index(p[0], p[1], p[3], 1 - p[2], (p[4] + hop) % NZ)) for p in places()],
            )
            for hop, part in zip(HOPS[start:], parts)
        ]

    pairs, side = block_pairs.T, xh.reshape(1)
    packed0 = pack(spectra, pairs, side, 0)
    packed1 = pack(spectra, pairs, side, 1)
    packed1, cosine, sine, where, halves = lax.optimization_barrier((packed1, cosine, sine, where, halves))
    landed0, theirs0 = exchange(packed0)
    own, other = first_half(where, landed0, theirs0, cosine[0], sine[0])
    landed1 = lax.all_to_all(packed1.reshape(128, 2, CH, FB), both, split_axis=0, concat_axis=0, tiled=True)
    landed1, own, other = lax.optimization_barrier((landed1, own, other))
    landed1 = landed1.reshape(16, 2, NZ, 2, CH, FB)
    def chunk(right, before, start, count):
        return second_half(where, landed1, right, cosine[1], sine[1], before, start, count)

    *pieces, mine1 = chunk(None, own, 0, NZ)
    theirs1 = swap(mine1)
    early = chunk(theirs1, other, 0, 3)
    theirs1, _ = lax.optimization_barrier((theirs1, early[0]))
    late = chunk(theirs1, other, 3, 1)
    first = send(pieces, 0)
    second = send(early, 0) + send(late, 3)
    filled = total(halves, 1, second, total(halves, 0, first))
    return jnp.transpose(filled, (0, 2, 1, 3))


def solution(mesh):
    in_specs = (P(None, "row", None, "col", None), P(), P("col"))
    out_specs = P("row", "col", None, None)
    return jax.shard_map(body, mesh=mesh, in_specs=in_specs, out_specs=out_specs, check_vma=False)
```
